256 devices in a mesh: replica: 32 (over x, z_hi, core), fsdp: 8 (over y, z_lo).
Axes of the slice: x: 4, y: 4, z: 8 (z_hi: 4, z_lo: 2; z = z_hi * 2 + z_lo), core: 2. Of those that a mesh axis runs over, the one named last changes fastest.
Arguments:
- tokens: bfloat16 [65536, 8192], P(('replica', 'fsdp')), may hold values from -6 to 6
- cotangent: bfloat16 [65536, 512], P(('replica', 'fsdp')), may hold values from -0.125 to 0.125
- gain: float32 [32, 8192], P('replica'), may hold values from 0.1 to 1.9
- value_weight: bfloat16 [32, 8192, 512], P('replica', 'fsdp'), may hold values from -0.25 to 0.25
- fragment: bfloat16 [32, 8192, 1024], P('replica', 'fsdp'), may hold values from -6 to 6
- global_table: float32 [4, 8192, 1024], P(None, ('fsdp', 'replica')), may hold values from -6 to 6
- momentum_table: float32 [4, 8192, 1024], P(None, ('fsdp', 'replica')), may hold values from -4 to 4
- frag_index: int32 [], replicated, may hold values from 0 to 3
Outputs:
- weight_grad: bfloat16 [32, 8192, 512], P('replica', 'fsdp')
- gain_grad: float32 [32, 8192], P('replica')
- new_fragment: bfloat16 [32, 8192, 1024], P('replica', 'fsdp')
- new_global: float32 [4, 8192, 1024], P(None, ('fsdp', 'replica'))
- new_momentum: float32 [4, 8192, 1024], P(None, ('fsdp', 'replica'))
The draws below stay inside these ranges and needn't reach their ends.
All inputs are finite; a program needn't handle non-finite values.
Results may differ from the reference program's by a relative error of at most 0.017.
Values may be sent and summed in bfloat16 or wider, within the bound.
A program may use at most 128 MiB of HBM per device.

```python
import jax
import jax.numpy as jnp
from jax import lax

D = 8192
VW = 512
KVW = 1024
NFRAG = 4
TOK_DEV = 256
REPLICAS = 32
TOK_REP = 2048
TOKENS = 65536
N_FSDP = 8


def block_scale(key, dims, cuts, low, largest):
    loudness = 1.0
    for position, blocks in cuts:
        draws = jax.random.uniform(jax.random.fold_in(jax.random.fold_in(key, 6), position), (blocks,), jnp.float32, low / len(cuts), largest / len(cuts))
        loudness = loudness * jnp.repeat(jnp.exp(draws), dims[position] // blocks).reshape((-1,) + (1,) * (len(dims) - 1 - position))
    return loudness


def gaussian(rng, extent, deviation, reach, shards=(), kind=jnp.bfloat16):
    loudness = block_scale(rng, extent, shards, -0.22, 0.18) if shards else 1.0
    entries = jax.random.normal(rng, extent, jnp.float32) * deviation * loudness
    return jnp.minimum(jnp.maximum(entries, -reach), reach).astype(kind)


def setup_inputs(seed: int = 0) -> dict:
    streams_of = jax.random.split(jax.random.key(seed), 9)
    tokens = gaussian(streams_of[0], (TOKENS, D), 1.0, 6.0, ((0, 256),))
    cotangent = gaussian(streams_of[1], (TOKENS, VW), (TOK_DEV * N_FSDP) ** -0.5, 0.125, ((0, 256),))
    gain = jnp.clip(1.0 + 0.18 * jax.random.normal(streams_of[2], (REPLICAS, D), jnp.float32), 0.1, 1.9)
    value_weight = gaussian(streams_of[3], (REPLICAS, D, VW), VW ** -0.5, 0.25, ((0, 32), (1, 8)))
    fragment = gaussian(streams_of[4], (REPLICAS, D, KVW), 1.0, 6.0, ((0, 32), (1, 8)))
    global_table = gaussian(streams_of[5], (NFRAG, D, KVW), 1.0, 6.0, ((1, 256),), jnp.float32)
    momentum_table = gaussian(streams_of[6], (NFRAG, D, KVW), 0.5, 4.0, ((1, 256),), jnp.float32)
    frag_index = jax.random.randint(streams_of[7], (), 0, NFRAG).astype(jnp.int32)
    return {"tokens": tokens, "cotangent": cotangent, "gain": gain, "value_weight": value_weight, "fragment": fragment, "global_table": global_table, "momentum_table": momentum_table, "frag_index": frag_index}


epsilon = 1e-05
outer_rate = 0.7
outer_beta = 0.9
mix_weight = 0.5

def replica_grads(inputs):
    rows, upstream, gains, weight = inputs
    floats = rows.astype(jnp.float32)
    inverse = lax.rsqrt(lax.optimization_barrier(jnp.mean(floats * floats, axis=-1, keepdims=True)) + epsilon)
    normed = floats * inverse
    scaled = (normed * gains).astype(jnp.bfloat16)
    blocks = scaled.reshape(N_FSDP, TOK_DEV, D).astype(jnp.float32)
    up_blocks = upstream.reshape(N_FSDP, TOK_DEV, VW).astype(jnp.float32)
    partials = jnp.einsum('ntd,ntv->ndv', blocks, up_blocks)
    partials = lax.optimization_barrier(partials.astype(jnp.bfloat16)).astype(jnp.float32)
    weight_grad = lax.optimization_barrier(jnp.sum(partials, axis=0)).astype(jnp.bfloat16)
    back = jnp.dot(upstream, weight.T, preferred_element_type=jnp.float32)
    gain_grad = lax.optimization_barrier(jnp.sum(normed * back, axis=0))
    return (weight_grad, gain_grad)

def reference(tokens, cotangent, gain, value_weight, fragment, global_table, momentum_table, frag_index):
    weight_grad, gain_grad = lax.map(replica_grads, (tokens.reshape(REPLICAS, TOK_REP, D), cotangent.reshape(REPLICAS, TOK_REP, VW), gain, value_weight))

    def add_one(index, total):
        return total + lax.dynamic_index_in_dim(fragment, index, 0, keepdims=False).astype(jnp.float32)
    summed = lax.fori_loop(0, REPLICAS, add_one, jnp.zeros((D, KVW), jnp.float32))
    mean_local = summed / REPLICAS
    chosen = lax.dynamic_index_in_dim(global_table, frag_index, 0, keepdims=False)
    velocity = lax.dynamic_index_in_dim(momentum_table, frag_index, 0, keepdims=False)
    delta = chosen - mean_local
    new_velocity = outer_beta * velocity + delta
    new_params = chosen - outer_rate * (delta + outer_beta * new_velocity)

    def blend(local):
        return (mix_weight * local.astype(jnp.float32) + (1.0 - mix_weight) * new_params).astype(jnp.bfloat16)
    new_fragment = lax.map(blend, fragment)
    new_global = lax.dynamic_update_index_in_dim(global_table, new_params, frag_index, 0)
    new_momentum = lax.dynamic_update_index_in_dim(momentum_table, new_velocity, frag_index, 0)
    return (weight_grad, gain_grad, new_fragment, new_global, new_momentum)
```

```python
import functools

import jax
import jax.numpy as jnp
from jax import lax
from jax.experimental import pallas as pl
from jax.experimental.pallas import tpu as pltpu
from jax.sharding import PartitionSpec as P

MESH = pl.DeviceIdType.MESH
F32 = jnp.float32
BF16 = jnp.bfloat16

epsilon = 1e-05
outer_rate = 0.7
outer_beta = 0.9
mix_weight = 0.5

NX, NZH, NC = 4, 4, 2
NY, NZL = 4, 2
TOK = 256
D = 8192
BLOCK = 1024
VW = 512
KVW = 1024
ROWS = 32
CHUNKS = 8
WIDTH = BLOCK // CHUNKS
HALVES = 2
HW = KVW // HALVES


def dot_rows(a, b):
    return lax.dot_general(a, b, (((0,), (0,)), ((), ())), preferred_element_type=F32)


def kernel(
    index_ref, tokens, cotangent, gain, weight, fragment, g_table, m_table,
    wg_out, gg_out, nf_out, ng_out, nm_out,
    tok_v, got, cot_v, cots, gain_v, weight_v, zs, zr, wg_v, gg_v,
    frag_v, frag_r, pair_v, xr, quad_v, zhr, params_v, nf_v, gt_v, mt_v, ng_v, nm_v,
    lsem, osem, tok_s, tok_r, cot_s, cot_r, z_s, z_r, gg_s, gg_r,
    fc_s, fc_r, xr_s, xr_r, zh_s, zh_r, az_s, az_r, ax_s, ax_r, ac_s, ac_r,
):
    rep = lax.axis_index("replica")
    fs = lax.axis_index("fsdp")
    x, zh, c = rep // (NZH * NC), (rep // NC) % NZH, rep % NC
    y, zl = fs // NZL, fs % NZL

    def device(dx=0, dzh=0, dc=0, dy=0, dz=0):
        return (
            (((x + dx) % NX) * NZH + (zh + dzh) % NZH) * NC + (c + dc) % NC,
            ((y + dy) % NY) * NZL + (zl + dz) % NZL,
        )

    def remote(src, dst, ssem, rsem, to):
        return pltpu.make_async_remote_copy(
            src_ref=src, dst_ref=dst, send_sem=ssem, recv_sem=rsem,
            device_id=to, device_id_type=MESH,
        )

    local = [
        pltpu.make_async_copy(src, dst, lsem.at[i])
        for i, (src, dst) in enumerate(
            (
                (tokens, tok_v),
                (cotangent, cot_v),
                (fragment, frag_v),
                (weight, weight_v),
                (gain, gain_v),
                (g_table, gt_v),
                (m_table, mt_v),
                (
                    tokens.at[:, pl.ds(pl.multiple_of(y * 2 * BLOCK, 2 * BLOCK), 2 * BLOCK)],
                    got.at[pl.ds(pl.multiple_of(y * TOK, TOK), TOK)],
                ),
            )
        )
    ]
    for i in (2, 0, 1, 7, 3, 4, 5, 6):
        local[i].start()

    partners = (
        [dict(dc=1)]
        + [dict(dx=d) for d in (1, 2, 3)]
        + [dict(dzh=d) for d in (1, 2, 3)]
        + [dict(dy=d) for d in (1, 2, 3)]
        + [dict(dz=1, dy=d) for d in range(4)]
    )
    barrier = pltpu.get_barrier_semaphore()
    for p in partners:
        pl.semaphore_signal(barrier, inc=1, device_id=device(**p), device_id_type=MESH)
    pl.semaphore_wait(barrier, len(partners))

    def half(h):
        return pl.ds(h * HW, HW)

    def core_sum(h):
        return remote(
            fragment.at[:, :, 1 - c, :, half(h)], frag_r.at[:, :, :, half(h)],
            fc_s.at[h], fc_r.at[h], device(dc=1),
        )

    def x_sum(h, d):
        return remote(
            pair_v.at[(x + d) % NX, :, :, half(h)], xr.at[d - 1, :, :, half(h)],
            xr_s.at[h, d - 1], xr_r.at[h, d - 1], device(dx=d),
        )

    def zh_sum(h, d):
        return remote(
            quad_v.at[(zh + d) % NZH, :, half(h)], zhr.at[d - 1, :, half(h)],
            zh_s.at[h, d - 1], zh_r.at[h, d - 1], device(dzh=d),
        )

    def zh_params(h, d):
        part = params_v.at[x, zh, c, :, half(h)]
        return remote(part, part, az_s.at[h, d - 1], az_r.at[h, d - 1], device(dzh=d))

    def x_params(h, d):
        part = params_v.at[x, :, c, :, half(h)]
        return remote(part, part, ax_s.at[h, d - 1], ax_r.at[h, d - 1], device(dx=d))

    def core_params(h):
        part = params_v.at[:, :, c, :, half(h)]
        return remote(part, part, ac_s.at[h], ac_r.at[h], device(dc=1))

    def token_part(k, b, d):
        where = ((y + d) % NY) * 2 * BLOCK + b * BLOCK + k * WIDTH
        return remote(
            tokens.at[:, pl.ds(pl.multiple_of(where, WIDTH), WIDTH)],
            got.at[
                pl.ds(pl.multiple_of(y * TOK, TOK), TOK),
                pl.ds(pl.multiple_of(b * BLOCK + k * WIDTH, WIDTH), WIDTH),
            ],
            tok_s.at[k, b, d - 1], tok_r.at[k, b, d - 1], device(dy=d),
        )

    def cot_part(d):
        part = cots.at[pl.ds(pl.multiple_of(y * TOK, TOK), TOK)]
        return remote(part, part, cot_s.at[d - 1], cot_r.at[d - 1], device(dy=d))

    def z_part(k):
        rows = pl.ds(pl.multiple_of(k * WIDTH, WIDTH), WIDTH)
        return remote(zs.at[rows], zr.at[rows], z_s.at[k], z_r.at[k], device(dz=1))

    def gain_part(i):
        part = gg_v.at[:, pl.ds(pl.multiple_of(fs * BLOCK, BLOCK), BLOCK)]
        return remote(part, part, gg_s.at[i - 1], gg_r.at[i - 1], device(dy=i // 2, dz=i % 2))

    def send_tokens(k):
        for b in (1 - zl, zl):
            for d in (2, 1, 3):
                token_part(k, b, d).start()

    for h in range(HALVES):
        core_sum(h).start()
    send_tokens(0)

    local[2].wait()
    for h in range(HALVES):
        core_sum(h).wait_recv()

        @pl.loop(0, NX * NZH)
        def _(i):
            i, j = i // NZH, i % NZH
            pair_v[i, j, :, half(h)] = (
                frag_v[i, j, c, :, half(h)].astype(F32) + frag_r[i, j, :, half(h)].astype(F32)
            ).astype(BF16)

        for d in (2, 1, 3):
            x_sum(h, d).start()

    local[0].wait()
    local[1].wait()

    @pl.loop(0, TOK // 16)
    def _(i):
        rows = pl.ds(pl.multiple_of(i * 16, 16), 16)
        part = tok_v[rows, :].astype(F32)
        inverse = lax.rsqrt(jnp.sum(part * part, axis=1, keepdims=True) / D + epsilon)
        cots[pl.ds(pl.multiple_of(y * TOK + i * 16, 16), 16), :] = (
            cot_v[rows, :].astype(F32) * inverse
        ).astype(BF16)

    for d in (2, 1, 3):
        cot_part(d).start()
    send_tokens(1)
    send_tokens(2)
    for i in (3, 4, 5, 6, 7):
        local[i].wait()

    def s2(h):
        for d in (1, 3, 2):
            x_sum(h, d).wait_recv()

        @pl.loop(0, NZH)
        def _(j):
            total = pair_v[x, j, :, half(h)].astype(F32)
            for d in (1, 2, 3):
                total = total + xr[d - 1, j, :, half(h)].astype(F32)
            quad_v[j, :, half(h)] = total.astype(BF16)

        for d in (2, 1, 3):
            zh_sum(h, d).start()

    def s3(h):
        for d in (1, 3, 2):
            zh_sum(h, d).wait_recv()
        total = quad_v[zh, :, half(h)].astype(F32)
        for d in (1, 2, 3):
            total = total + zhr[d - 1, :, half(h)].astype(F32)
        picked = index_ref[0]
        chosen = gt_v[picked, :, half(h)]
        velocity = mt_v[picked, :, half(h)]
        delta = chosen - total / (NX * NZH * NC)
        new_velocity = outer_beta * velocity + delta
        new_params = chosen - outer_rate * (delta + outer_beta * new_velocity)
        params_v[x, zh, c, :, half(h)] = new_params.astype(BF16)
        for d in (2, 1, 3):
            zh_params(h, d).start()
        for i in range(4):
            ng_v[i, :, half(h)] = jnp.where(picked == i, new_params, gt_v[i, :, half(h)])
            nm_v[i, :, half(h)] = jnp.where(picked == i, new_velocity, mt_v[i, :, half(h)])
        if h == HALVES - 1:
            pltpu.make_async_copy(ng_v, ng_out, osem.at[2]).start()
            pltpu.make_async_copy(nm_v, nm_out, osem.at[3]).start()

    def s4(h):
        for d in (1, 3, 2):
            zh_params(h, d).wait_recv()
        for d in (2, 1, 3):
            x_params(h, d).start()

    def s5(h):
        for d in (1, 3, 2):
            x_params(h, d).wait_recv()
        core_params(h).start()

    def s6(h):
        core_params(h).wait_recv()

        @pl.loop(0, NX * NZH)
        def _(i):
            i, j = i // NZH, i % NZH
            nf_v[i, j, :, :, half(h)] = (
                mix_weight * frag_v[i, j, :, :, half(h)].astype(F32)
                + (1.0 - mix_weight) * params_v[i, j, :, :, half(h)].astype(F32)
            ).astype(BF16)

        pltpu.make_async_copy(
            nf_v.at[:, :, :, :, half(h)], nf_out.at[:, :, :, :, half(h)], osem.at[h]
        ).start()

    def wg_copy(k):
        rows = pl.ds(pl.multiple_of(k * WIDTH, WIDTH), WIDTH)
        return pltpu.make_async_copy(wg_v.at[rows], wg_out.at[rows], osem.at[4 + k])

    for d in (1, 3, 2):
        cot_part(d).wait_recv()

    steps = {
        0: [(s2, 0)],
        1: [(s2, 1), (s3, 0)],
        2: [(s4, 0), (s3, 1)],
        3: [(s5, 0), (s4, 1)],
        4: [(s6, 0), (s5, 1)],
        5: [(s6, 1)],
    }

    @pl.loop(0, CHUNKS + 1)
    def _(k):
        @pl.when(k < CHUNKS)
        def _():
            for d in (1, 3, 2):
                token_part(k, 1 - zl, d).wait_recv()

            @pl.when(k + 3 < CHUNKS)
            def _():
                send_tokens(k + 3)

            cols = pl.ds(pl.multiple_of((1 - zl) * BLOCK + k * WIDTH, WIDTH), WIDTH)
            zs[pl.ds(pl.multiple_of(k * WIDTH, WIDTH), WIDTH), :] = dot_rows(
                got[:, cols], cots[...]
            ).astype(BF16)
            z_part(k).start()
            for d in (1, 3, 2):
                token_part(k, zl, d).wait_recv()

        @pl.when(k > 0)
        def _():
            j = k - 1
            rows = pl.ds(pl.multiple_of(j * WIDTH, WIDTH), WIDTH)
            cols = pl.ds(pl.multiple_of(zl * BLOCK + j * WIDTH, WIDTH), WIDTH)
            mine = dot_rows(got[:, cols], cots[...])
            z_part(j).wait_recv()
            total = mine + zr[rows, :].astype(F32)
            where = pl.ds(pl.multiple_of(fs * BLOCK + j * WIDTH, WIDTH), WIDTH)
            gains = jnp.broadcast_to(gain_v[:, where], (128, WIDTH)).T
            wg_v[rows, :] = (total * jnp.concatenate([gains] * (VW // 128), axis=1)).astype(BF16)
            wg_copy(j).start()
            terms = total * weight_v[rows, :].astype(F32)
            terms = sum(terms[:, i * 128 : (i + 1) * 128] for i in range(VW // 128))
            gg_v[:, where] = jnp.sum(terms.T, axis=0, keepdims=True)

        for at, calls in steps.items():

            @pl.when(k == at)
            def _():
                for step, h in calls:
                    step(h)

    for i in (7, 3, 5, 4, 6, 2, 1):
        gain_part(i).start()

    for h in range(HALVES):
        core_sum(h).wait_send()
        core_params(h).wait_send()
        for d in (1, 2, 3):
            for part in (x_sum, zh_sum, zh_params, x_params):
                part(h, d).wait_send()
        pltpu.make_async_copy(
            nf_v.at[:, :, :, :, half(h)], nf_out.at[:, :, :, :, half(h)], osem.at[h]
        ).wait()
    pltpu.make_async_copy(ng_v, ng_out, osem.at[2]).wait()
    pltpu.make_async_copy(nm_v, nm_out, osem.at[3]).wait()
    for d in (1, 2, 3):
        cot_part(d).wait_send()

    @pl.loop(0, CHUNKS)
    def _(k):
        for b in (0, 1):
            for d in (1, 2, 3):
                token_part(k, b, d).wait_send()
        z_part(k).wait_send()
        wg_copy(k).wait()

    for i in range(1, 8):
        gain_part(i).wait_recv()
    last = pltpu.make_async_copy(gg_v, gg_out, lsem.at[8])
    last.start()
    for i in range(1, 8):
        gain_part(i).wait_send()
    last.wait()


def body(tokens, cotangent, gain, value_weight, fragment, global_table, momentum_table, frag_index):
    grid = (NX, NZH, NC, ROWS, KVW)
    dma = pltpu.SemaphoreType.DMA
    any_space = pl.BlockSpec(memory_space=pl.ANY)
    wg, gg, nf, ng, nm = pl.pallas_call(
        kernel,
        out_shape=(
            jax.ShapeDtypeStruct((BLOCK, VW), BF16),
            jax.ShapeDtypeStruct((1, D), F32),
            jax.ShapeDtypeStruct(grid, BF16),
            jax.ShapeDtypeStruct((4, ROWS, KVW), F32),
            jax.ShapeDtypeStruct((4, ROWS, KVW), F32),
        ),
        in_specs=[pl.BlockSpec(memory_space=pltpu.SMEM)] + [any_space] * 7,
        out_specs=[any_space] * 5,
        scratch_shapes=[
            pltpu.VMEM((TOK, D), BF16),
            pltpu.VMEM((NY * TOK, 2 * BLOCK), BF16),
            pltpu.VMEM((TOK, VW), BF16),
            pltpu.VMEM((NY * TOK, VW), BF16),
            pltpu.VMEM((1, D), F32),
            pltpu.VMEM((BLOCK, VW), BF16),
            pltpu.VMEM((BLOCK, VW), BF16),
            pltpu.VMEM((BLOCK, VW), BF16),
            pltpu.VMEM((BLOCK, VW), BF16),
            pltpu.VMEM((1, D), F32),
            pltpu.VMEM(grid, BF16),
            pltpu.VMEM((NX, NZH, ROWS, KVW), BF16),
            pltpu.VMEM((NX, NZH, ROWS, KVW), BF16),
            pltpu.VMEM((NX - 1, NZH, ROWS, KVW), BF16),
            pltpu.VMEM((NZH, ROWS, KVW), BF16),
            pltpu.VMEM((NZH - 1, ROWS, KVW), BF16),
            pltpu.VMEM(grid, BF16),
            pltpu.VMEM(grid, BF16),
        ]
        + [pltpu.VMEM((4, ROWS, KVW), F32)] * 4
        + [
            dma((9,)),
            dma((4 + CHUNKS,)),
        ]
        + [dma((CHUNKS, 2, 3))] * 2
        + [dma((3,))] * 2
        + [dma((CHUNKS,))] * 2
        + [dma((7,))] * 2
        + [dma((HALVES,))] * 2
        + [dma((HALVES, 3))] * 8
        + [dma((HALVES,))] * 2,
        compiler_params=pltpu.CompilerParams(
            collective_id=0, has_side_effects=True, vmem_limit_bytes=48 << 20
        ),
        cost_estimate=pl.CostEstimate(
            flops=2 * 2 * TOK * D * VW, bytes_accessed=16 << 20, transcendentals=TOK
        ),
        name="round",
    )(
        frag_index.reshape(1),
        tokens,
        cotangent,
        gain,
        value_weight.reshape(BLOCK, VW),
        fragment.reshape(grid),
        global_table,
        momentum_table,
    )
    return wg[None], gg, nf.reshape(1, BLOCK, KVW), ng, nm


def solution(mesh):
    placed = (
        P(("replica", "fsdp"), None),
        P(("replica", "fsdp"), None),
        P("replica", None),
        P("replica", "fsdp", None),
        P("replica", "fsdp", None),
        P(None, ("fsdp", "replica"), None),
        P(None, ("fsdp", "replica"), None),
        P(),
    )
    return jax.shard_map(
        body,
        mesh=mesh,
        in_specs=placed,
        out_specs=(
            P("replica", "fsdp", None),
            P("replica", None),
            P("replica", "fsdp", None),
            P(None, ("fsdp", "replica"), None),
            P(None, ("fsdp", "replica"), None),
        ),
        check_vma=False,
    )
```

```python
import functools

import jax
import jax.numpy as jnp
from jax import lax
from jax.experimental import pallas as pl
from jax.experimental.pallas import tpu as pltpu
from jax.sharding import PartitionSpec as P

MESH = pl.DeviceIdType.MESH
F32 = jnp.float32
BF16 = jnp.bfloat16

epsilon = 1e-05
outer_rate = 0.7
outer_beta = 0.9
mix_weight = 0.5

NX, NZH, NC = 4, 4, 2
NY, NZL = 4, 2
TOK = 256
D = 8192
BLOCK = 1024
VW = 512
KVW = 1024
ROWS = 32
CHUNKS = 8
WIDTH = BLOCK // CHUNKS
AHEAD = 4
LAG = 3
HALVES = 2
HW = KVW // HALVES


def dot_rows(a, b):
    return lax.dot_general(a, b, (((0,), (0,)), ((), ())), preferred_element_type=F32)


def kernel(
    index_ref, tokens, cotangent, gain, weight, fragment, g_table, m_table,
    wg_out, gg_out, nf_out, ng_out, nm_out,
    tok_v, far_v, near_v, part_s, part_v, cot_v, cot_own, cot_near, gain_v, weight_v, zs, zr, wg_v, gg_v,
    frag_v, frag_r, pair_v, xr, quad_v, zhr, params_v, nf_v, gt_v, mt_v, ng_v, nm_v,
    lsem, osem, far_s, far_r, near_s, near_r, part_ss, part_rs, cot_s, cot_r, z_s, z_r, gg_s, gg_r,
    fc_s, fc_r, xr_s, xr_r, zh_s, zh_r, az_s, az_r, ax_s, ax_r, ac_s, ac_r,
):
    rep = lax.axis_index("replica")
    fs = lax.axis_index("fsdp")
    x, zh, c = rep // (NZH * NC), (rep // NC) % NZH, rep % NC
    y, zl = fs // NZL, fs % NZL

    def device(dx=0, dzh=0, dc=0, dy=0, dz=0):
        return (
            (((x + dx) % NX) * NZH + (zh + dzh) % NZH) * NC + (c + dc) % NC,
            ((y + dy) % NY) * NZL + (zl + dz) % NZL,
        )

    def remote(src, dst, ssem, rsem, to):
        return pltpu.make_async_remote_copy(
            src_ref=src, dst_ref=dst, send_sem=ssem, recv_sem=rsem,
            device_id=to, device_id_type=MESH,
        )

    local = [
        pltpu.make_async_copy(src, dst, lsem.at[i])
        for i, (src, dst) in enumerate(
            (
                (tokens, tok_v),
                (cotangent, cot_v),
                (fragment, frag_v),
                (weight, weight_v),
                (gain, gain_v),
                (g_table, gt_v),
                (m_table, mt_v),
            )
        )
    ]
    for i in (2, 0, 1, 3, 4, 5, 6):
        local[i].start()

    partners = (
        [dict(dc=1)]
        + [dict(dx=d) for d in (1, 2, 3)]
        + [dict(dzh=d) for d in (1, 2, 3)]
        + [dict(dy=d) for d in (1, 2, 3)]
        + [dict(dz=1, dy=d) for d in range(4)]
    )
    barrier = pltpu.get_barrier_semaphore()
    for p in partners:
        pl.semaphore_signal(barrier, inc=1, device_id=device(**p), device_id_type=MESH)
    pl.semaphore_wait(barrier, len(partners))

    def half(h):
        return pl.ds(h * HW, HW)

    def core_sum(h):
        return remote(
            fragment.at[:, :, 1 - c, :, half(h)], frag_r.at[:, :, :, half(h)],
            fc_s.at[h], fc_r.at[h], device(dc=1),
        )

    def x_sum(h, d):
        return remote(
            pair_v.at[(x + d) % NX, :, :, half(h)], xr.at[d - 1, :, :, half(h)],
            xr_s.at[h, d - 1], xr_r.at[h, d - 1], device(dx=d),
        )

    def zh_sum(h, d):
        return remote(
            quad_v.at[(zh + d) % NZH, :, half(h)], zhr.at[d - 1, :, half(h)],
            zh_s.at[h, d - 1], zh_r.at[h, d - 1], device(dzh=d),
        )

    def zh_params(h, d):
        part = params_v.at[x, zh, c, :, half(h)]
        return remote(part, part, az_s.at[h, d - 1], az_r.at[h, d - 1], device(dzh=d))

    def x_params(h, d):
        part = params_v.at[x, :, c, :, half(h)]
        return remote(part, part, ax_s.at[h, d - 1], ax_r.at[h, d - 1], device(dx=d))

    def core_params(h):
        part = params_v.at[:, :, c, :, half(h)]
        return remote(part, part, ac_s.at[h], ac_r.at[h], device(dc=1))

    def at(b, k):
        return pl.ds(pl.multiple_of(b * BLOCK + k * WIDTH, WIDTH), WIDTH)

    def owned(d, b, k):
        return pl.ds(
            pl.multiple_of(((y + d) % NY) * 2 * BLOCK + b * BLOCK + k * WIDTH, WIDTH), WIDTH
        )

    def side(k):
        return 1 - 2 * (k % 2)

    def far_part(o, b, k):
        return remote(
            tokens.at[:, owned(2, b, k)], far_v.at[:, at(b, k)],
            far_s.at[o, k], far_r.at[o, k], device(dy=NY - side(k)),
        )

    def near_part(o, b, k):
        return remote(
            tokens.at[:, owned(NY + side(k), b, k)], near_v.at[:, at(b, k)],
            near_s.at[o, k], near_r.at[o, k], device(dy=NY + side(k)),
        )

    def product_part(o, b, k):
        return remote(
            part_s.at[at(b, k)], part_v.at[at(b, k)],
            part_ss.at[o, k], part_rs.at[o, k], device(dy=NY - side(k)),
        )

    def cot_part(i):
        return remote(
            cot_own, cot_near.at[1 - i], cot_s.at[i], cot_r.at[1 - i], device(dy=1 + 2 * i)
        )

    def chunk(q):
        first, last, odd = 1 - (q + 2 * CHUNKS - 1) // (2 * CHUNKS), (q + 1) // (2 * CHUNKS), q % 2
        o = (1 - odd) * (1 - first) + last
        k = odd * ((q + 1) // 2 - last) + (1 - odd) * (q // 2 - 1 + first)
        return o, o * zl + (1 - o) * (1 - zl), k

    def z_part(k):
        rows = pl.ds(pl.multiple_of(k * WIDTH, WIDTH), WIDTH)
        return remote(zs.at[rows], zr.at[rows], z_s.at[k], z_r.at[k], device(dz=1))

    def gain_part(i):
        part = gg_v.at[:, pl.ds(pl.multiple_of(fs * BLOCK, BLOCK), BLOCK)]
        return remote(part, part, gg_s.at[i - 1], gg_r.at[i - 1], device(dy=i // 2, dz=i % 2))

    for h in range(HALVES):
        core_sum(h).start()

    @pl.loop(0, CHUNKS)
    def _(q):
        far_part(*chunk(q)).start()


    local[2].wait()
    for h in range(HALVES):
        core_sum(h).wait_recv()

        @pl.loop(0, NX * NZH)
        def _(i):
            i, j = i // NZH, i % NZH
            pair_v[i, j, :, half(h)] = (
                frag_v[i, j, c, :, half(h)].astype(F32) + frag_r[i, j, :, half(h)].astype(F32)
            ).astype(BF16)

        for d in (2, 1, 3):
            x_sum(h, d).start()

    local[0].wait()
    local[1].wait()

    @pl.loop(0, TOK // 16)
    def _(i):
        rows = pl.ds(pl.multiple_of(i * 16, 16), 16)
        part = tok_v[rows, :].astype(F32)
        inverse = lax.rsqrt(jnp.sum(part * part, axis=1, keepdims=True) / D + epsilon)
        cot_own[rows, :] = (cot_v[rows, :].astype(F32) * inverse).astype(BF16)

    for i in (0, 1):
        cot_part(i).start()

    @pl.loop(CHUNKS, 2 * CHUNKS)
    def _(q):
        far_part(*chunk(q)).start()

    @pl.loop(0, AHEAD)
    def _(q):
        near_part(*chunk(q)).start()

    for i in (3, 4, 5, 6):
        local[i].wait()

    def s2(h):
        for d in (1, 3, 2):
            x_sum(h, d).wait_recv()

        @pl.loop(0, NZH)
        def _(j):
            total = pair_v[x, j, :, half(h)].astype(F32)
            for d in (1, 2, 3):
                total = total + xr[d - 1, j, :, half(h)].astype(F32)
            quad_v[j, :, half(h)] = total.astype(BF16)

        for d in (2, 1, 3):
            zh_sum(h, d).start()

    def s3(h):
        for d in (1, 3, 2):
            zh_sum(h, d).wait_recv()
        total = quad_v[zh, :, half(h)].astype(F32)
        for d in (1, 2, 3):
            total = total + zhr[d - 1, :, half(h)].astype(F32)
        picked = index_ref[0]
        chosen = gt_v[picked, :, half(h)]
        velocity = mt_v[picked, :, half(h)]
        delta = chosen - total / (NX * NZH * NC)
        new_velocity = outer_beta * velocity + delta
        new_params = chosen - outer_rate * (delta + outer_beta * new_velocity)
        params_v[x, zh, c, :, half(h)] = new_params.astype(BF16)
        for d in (2, 1, 3):
            zh_params(h, d).start()
        for i in range(4):
            ng_v[i, :, half(h)] = jnp.where(picked == i, new_params, gt_v[i, :, half(h)])
            nm_v[i, :, half(h)] = jnp.where(picked == i, new_velocity, mt_v[i, :, half(h)])
        if h == HALVES - 1:
            pltpu.make_async_copy(ng_v, ng_out, osem.at[2]).start()
            pltpu.make_async_copy(nm_v, nm_out, osem.at[3]).start()

    def s4(h):
        for d in (1, 3, 2):
            zh_params(h, d).wait_recv()
        for d in (2, 1, 3):
            x_params(h, d).start()

    def s5(h):
        for d in (1, 3, 2):
            x_params(h, d).wait_recv()
        core_params(h).start()

    def s6(h):
        core_params(h).wait_recv()

        @pl.loop(0, NX * NZH)
        def _(i):
            i, j = i // NZH, i % NZH
            nf_v[i, j, :, :, half(h)] = (
                mix_weight * frag_v[i, j, :, :, half(h)].astype(F32)
                + (1.0 - mix_weight) * params_v[i, j, :, :, half(h)].astype(F32)
            ).astype(BF16)

        pltpu.make_async_copy(
            nf_v.at[:, :, :, :, half(h)], nf_out.at[:, :, :, :, half(h)], osem.at[h]
        ).start()

    def wg_copy(k):
        rows = pl.ds(pl.multiple_of(k * WIDTH, WIDTH), WIDTH)
        return pltpu.make_async_copy(wg_v.at[rows], wg_out.at[rows], osem.at[4 + k])

    for i in (0, 1):
        cot_part(1 - i).wait_recv()

    def combine(q):
        o, b, k = chunk(q)
        far_part(o, b, k).wait_recv()
        part_s[at(b, k), :] = (
            dot_rows(tok_v[:, owned(NY - side(k), b, k)], cot_own[...])
            + dot_rows(far_v[:, at(b, k)], cot_near[k % 2])
        ).astype(BF16)
        product_part(o, b, k).start()

    def collect(o, b, k):
        near_part(o, b, k).wait_recv()
        mine = dot_rows(tok_v[:, owned(0, b, k)], cot_own[...]) + dot_rows(
            near_v[:, at(b, k)], cot_near[1 - k % 2]
        )
        product_part(o, b, k).wait_recv()
        return mine + part_v[at(b, k), :].astype(F32)

    def finish(q):
        o, _, k = chunk(q)
        rows = pl.ds(pl.multiple_of(k * WIDTH, WIDTH), WIDTH)

        @pl.when(o == 0)
        def _():
            zs[rows, :] = collect(o, 1 - zl, k).astype(BF16)
            z_part(k).start()

        @pl.when(o == 1)
        def _():
            mine = collect(o, zl, k)
            z_part(k).wait_recv()
            total = mine + zr[rows, :].astype(F32)
            where = pl.ds(pl.multiple_of(fs * BLOCK + k * WIDTH, WIDTH), WIDTH)
            gains = jnp.broadcast_to(gain_v[:, where], (128, WIDTH)).T
            wg_v[rows, :] = (total * jnp.concatenate([gains] * (VW // 128), axis=1)).astype(BF16)
            wg_copy(k).start()
            terms = total * weight_v[rows, :].astype(F32)
            terms = sum(terms[:, i * 128 : (i + 1) * 128] for i in range(VW // 128))
            gg_v[:, where] = jnp.sum(terms.T, axis=0, keepdims=True)

    steps = {
        0: [(s2, 0)],
        2: [(s2, 1)],
        3: [(s3, 0)],
        5: [(s3, 1)],
        6: [(s4, 0)],
        8: [(s4, 1)],
        10: [(s5, 0)],
        12: [(s5, 1)],
        14: [(s6, 0)],
        16: [(s6, 1)],
    }

    @pl.loop(0, 2 * CHUNKS + LAG)
    def _(q):
        @pl.when(q < 2 * CHUNKS)
        def _():
            combine(q)

            @pl.when(q + AHEAD < 2 * CHUNKS)
            def _():
                near_part(*chunk(q + AHEAD)).start()

        @pl.when(q >= LAG)
        def _():
            finish(q - LAG)

        for when, calls in steps.items():

            @pl.when(q == when)
            def _():
                for step, h in calls:
                    step(h)

    for i in (7, 3, 5, 4, 6, 2, 1):
        gain_part(i).start()

    for h in range(HALVES):
        core_sum(h).wait_send()
        core_params(h).wait_send()
        for d in (1, 2, 3):
            for part in (x_sum, zh_sum, zh_params, x_params):
                part(h, d).wait_send()
        pltpu.make_async_copy(
            nf_v.at[:, :, :, :, half(h)], nf_out.at[:, :, :, :, half(h)], osem.at[h]
        ).wait()
    pltpu.make_async_copy(ng_v, ng_out, osem.at[2]).wait()
    pltpu.make_async_copy(nm_v, nm_out, osem.at[3]).wait()
    for i in (0, 1):
        cot_part(i).wait_send()

    @pl.loop(0, CHUNKS)
    def _(k):
        for o in (0, 1):
            for part in (far_part, near_part, product_part):
                part(o, o, k).wait_send()
        z_part(k).wait_send()
        wg_copy(k).wait()

    for i in range(1, 8):
        gain_part(i).wait_recv()
    last = pltpu.make_async_copy(gg_v, gg_out, lsem.at[8])
    last.start()
    for i in range(1, 8):
        gain_part(i).wait_send()
    last.wait()


def store(*refs):
    found, out, held, came, went = refs[:5], refs[5:10], refs[10:15], refs[15], refs[16]
    loads = [pltpu.make_async_copy(found[i], held[i], came.at[i]) for i in range(5)]
    stores = [pltpu.make_async_copy(held[i], out[i], went.at[i]) for i in range(5)]
    for i in range(5):
        loads[i].start()
    for i in range(5):
        loads[i].wait()
        stores[i].start()
    for i in range(5):
        stores[i].wait()


def body(tokens, cotangent, gain, value_weight, fragment, global_table, momentum_table, frag_index):
    grid = (NX, NZH, NC, ROWS, KVW)
    dma = pltpu.SemaphoreType.DMA
    any_space = pl.BlockSpec(memory_space=pl.ANY)
    results = (
        jax.ShapeDtypeStruct((BLOCK, VW), BF16),
        jax.ShapeDtypeStruct((1, D), F32),
        jax.ShapeDtypeStruct(grid, BF16),
        jax.ShapeDtypeStruct((4, ROWS, KVW), F32),
        jax.ShapeDtypeStruct((4, ROWS, KVW), F32),
    )
    found = pl.pallas_call(
        kernel,
        out_shape=results,
        in_specs=[pl.BlockSpec(memory_space=pltpu.SMEM)] + [any_space] * 7,
        out_specs=[any_space] * 5,
        scratch_shapes=[
            pltpu.VMEM((TOK, D), BF16),
            pltpu.VMEM((TOK, 2 * BLOCK), BF16),
            pltpu.VMEM((TOK, 2 * BLOCK), BF16),
            pltpu.VMEM((2 * BLOCK, VW), BF16),
            pltpu.VMEM((2 * BLOCK, VW), BF16),
            pltpu.VMEM((TOK, VW), BF16),
            pltpu.VMEM((TOK, VW), BF16),
            pltpu.VMEM((2, TOK, VW), BF16),
            pltpu.VMEM((1, D), F32),
            pltpu.VMEM((BLOCK, VW), BF16),
            pltpu.VMEM((BLOCK, VW), BF16),
            pltpu.VMEM((BLOCK, VW), BF16),
            pltpu.VMEM((BLOCK, VW), BF16),
            pltpu.VMEM((1, D), F32),
            pltpu.VMEM(grid, BF16),
            pltpu.VMEM((NX, NZH, ROWS, KVW), BF16),
            pltpu.VMEM((NX, NZH, ROWS, KVW), BF16),
            pltpu.VMEM((NX - 1, NZH, ROWS, KVW), BF16),
            pltpu.VMEM((NZH, ROWS, KVW), BF16),
            pltpu.VMEM((NZH - 1, ROWS, KVW), BF16),
            pltpu.VMEM(grid, BF16),
            pltpu.VMEM(grid, BF16),
        ]
        + [pltpu.VMEM((4, ROWS, KVW), F32)] * 4
        + [
            dma((9,)),
            dma((4 + CHUNKS,)),
        ]
        + [dma((2, CHUNKS))] * 6
        + [dma((2,))] * 2
        + [dma((CHUNKS,))] * 2
        + [dma((7,))] * 2
        + [dma((HALVES,))] * 2
        + [dma((HALVES, 3))] * 8
        + [dma((HALVES,))] * 2,
        compiler_params=pltpu.CompilerParams(
            collective_id=0, has_side_effects=True, vmem_limit_bytes=60 << 20
        ),
        cost_estimate=pl.CostEstimate(
            flops=2 * 2 * TOK * D * VW, bytes_accessed=16 << 20, transcendentals=TOK
        ),
        name="round",
    )(
        frag_index.reshape(1),
        tokens,
        cotangent,
        gain,
        value_weight.reshape(BLOCK, VW),
        fragment.reshape(grid),
        global_table,
        momentum_table,
    )
    wg, gg, nf, ng, nm = pl.pallas_call(
        store,
        out_shape=results,
        in_specs=[any_space] * 5,
        out_specs=[any_space] * 5,
        scratch_shapes=[pltpu.VMEM(r.shape, r.dtype) for r in results] + [dma((5,))] * 2,
        compiler_params=pltpu.CompilerParams(vmem_limit_bytes=60 << 20),
        name="store",
    )(*found)
    return wg[None], gg, nf.reshape(1, BLOCK, KVW), ng, nm


def solution(mesh):
    placed = (
        P(("replica", "fsdp"), None),
        P(("replica", "fsdp"), None),
        P("replica", None),
        P("replica", "fsdp", None),
        P("replica", "fsdp", None),
        P(None, ("fsdp", "replica"), None),
        P(None, ("fsdp", "replica"), None),
        P(),
    )
    return jax.shard_map(
        body,
        mesh=mesh,
        in_specs=placed,
        out_specs=(
            P("replica", "fsdp", None),
            P("replica", None),
            P("replica", "fsdp", None),
            P(None, ("fsdp", "replica"), None),
            P(None, ("fsdp", "replica"), None),
        ),
        check_vma=False,
    )
```

```python
import functools

import jax
import jax.numpy as jnp
from jax import lax
from jax.experimental import pallas as pl
from jax.experimental.pallas import tpu as pltpu
from jax.sharding import PartitionSpec as P

MESH = pl.DeviceIdType.MESH
F32 = jnp.float32
BF16 = jnp.bfloat16

epsilon = 1e-05
outer_rate = 0.7
outer_beta = 0.9
mix_weight = 0.5

NX, NZH, NC = 4, 4, 2
NY, NZL = 4, 2
TOK = 256
D = 8192
BLOCK = 1024
VW = 512
KVW = 1024
ROWS = 32
CHUNKS = 8
WIDTH = BLOCK // CHUNKS
AHEAD = 2
LAG = 4
HALVES = 2
HW = KVW // HALVES


def dot_rows(a, b):
    return lax.dot_general(a, b, (((0,), (0,)), ((), ())), preferred_element_type=F32)


def kernel(
    index_ref, tokens, cotangent, gain, weight, fragment, g_table, m_table,
    wg_v, gg_v, nf_v, ng_v, nm_v,
    tok_v, far_v, near_v, part_s, part_v, cot_v, cot_own, cot_near, gain_v, weight_v, zs, zr,
    frag_v, frag_r, pair_v, xr, quad_v, zhr, params_v, gt_v, mt_v,
    lsem, far_s, far_r, near_s, near_r, part_ss, part_rs, cot_s, cot_r, z_s, z_r, gg_s, gg_r,
    fc_s, fc_r, xr_s, xr_r, zh_s, zh_r, az_s, az_r, ax_s, ax_r, ac_s, ac_r,
):
    rep = lax.axis_index("replica")
    fs = lax.axis_index("fsdp")
    x, zh, c = rep // (NZH * NC), (rep // NC) % NZH, rep % NC
    y, zl = fs // NZL, fs % NZL

    def device(dx=0, dzh=0, dc=0, dy=0, dz=0):
        return (
            (((x + dx) % NX) * NZH + (zh + dzh) % NZH) * NC + (c + dc) % NC,
            ((y + dy) % NY) * NZL + (zl + dz) % NZL,
        )

    def remote(src, dst, ssem, rsem, to):
        return pltpu.make_async_remote_copy(
            src_ref=src, dst_ref=dst, send_sem=ssem, recv_sem=rsem,
            device_id=to, device_id_type=MESH,
        )

    local = [
        pltpu.make_async_copy(src, dst, lsem.at[i])
        for i, (src, dst) in enumerate(
            (
                (tokens, tok_v),
                (cotangent, cot_v),
                (fragment, frag_v),
                (weight, weight_v),
                (gain, gain_v),
                (g_table, gt_v),
                (m_table, mt_v),
            )
        )
    ]
    for i in (2, 0, 1, 3, 4, 5, 6):
        local[i].start()

    partners = (
        [dict(dc=1)]
        + [dict(dx=d) for d in (1, 2, 3)]
        + [dict(dzh=d) for d in (1, 2, 3)]
        + [dict(dy=d) for d in (1, 2, 3)]
        + [dict(dz=1, dy=d) for d in range(4)]
    )
    barrier = pltpu.get_barrier_semaphore()
    for p in partners:
        pl.semaphore_signal(barrier, inc=1, device_id=device(**p), device_id_type=MESH)
    pl.semaphore_wait(barrier, len(partners))

    def half(h):
        return pl.ds(h * HW, HW)

    def core_sum(h):
        return remote(
            fragment.at[:, :, 1 - c, :, half(h)], frag_r.at[:, :, :, half(h)],
            fc_s.at[h], fc_r.at[h], device(dc=1),
        )

    def x_sum(h, d):
        return remote(
            pair_v.at[(x + d) % NX, :, :, half(h)], xr.at[d - 1, :, :, half(h)],
            xr_s.at[h, d - 1], xr_r.at[h, d - 1], device(dx=d),
        )

    def zh_sum(h, d):
        return remote(
            quad_v.at[(zh + d) % NZH, :, half(h)], zhr.at[d - 1, :, half(h)],
            zh_s.at[h, d - 1], zh_r.at[h, d - 1], device(dzh=d),
        )

    def zh_params(h, d):
        part = params_v.at[x, zh, c, :, half(h)]
        return remote(part, part, az_s.at[h, d - 1], az_r.at[h, d - 1], device(dzh=d))

    def x_params(h, d):
        part = params_v.at[x, :, c, :, half(h)]
        return remote(part, part, ax_s.at[h, d - 1], ax_r.at[h, d - 1], device(dx=d))

    def core_params(h):
        part = params_v.at[:, :, c, :, half(h)]
        return remote(part, part, ac_s.at[h], ac_r.at[h], device(dc=1))

    def at(b, k):
        return pl.ds(pl.multiple_of(b * BLOCK + k * WIDTH, WIDTH), WIDTH)

    def owned(d, b, k):
        return pl.ds(
            pl.multiple_of(((y + d) % NY) * 2 * BLOCK + b * BLOCK + k * WIDTH, WIDTH), WIDTH
        )

    def side(k):
        return 1 - 2 * (k % 2)

    def far_part(o, b, k):
        return remote(
            tokens.at[:, owned(2, b, k)], far_v.at[:, at(b, k)],
            far_s.at[o, k], far_r.at[o, k], device(dy=NY - side(k)),
        )

    def near_part(o, b, k):
        return remote(
            tokens.at[:, owned(NY + side(k), b, k)], near_v.at[:, at(b, k)],
            near_s.at[o, k], near_r.at[o, k], device(dy=NY + side(k)),
        )

    def product_part(o, b, k):
        return remote(
            part_s.at[at(b, k)], part_v.at[at(b, k)],
            part_ss.at[o, k], part_rs.at[o, k], device(dy=NY - side(k)),
        )

    def cot_part(i):
        return remote(
            cot_own, cot_near.at[1 - i], cot_s.at[i], cot_r.at[1 - i], device(dy=1 + 2 * i)
        )

    def chunk(q):
        first, last, odd = 1 - (q + 2 * CHUNKS - 1) // (2 * CHUNKS), (q + 1) // (2 * CHUNKS), q % 2
        o = (1 - odd) * (1 - first) + last
        k = odd * ((q + 1) // 2 - last) + (1 - odd) * (q // 2 - 1 + first)
        return o, o * zl + (1 - o) * (1 - zl), k

    def z_part(k):
        rows = pl.ds(pl.multiple_of(k * WIDTH, WIDTH), WIDTH)
        return remote(zs.at[rows], zr.at[rows], z_s.at[k], z_r.at[k], device(dz=1))

    def gain_part(i):
        part = gg_v.at[:, pl.ds(pl.multiple_of(fs * BLOCK, BLOCK), BLOCK)]
        return remote(part, part, gg_s.at[i - 1], gg_r.at[i - 1], device(dy=i // 2, dz=i % 2))

    for h in range(HALVES):
        core_sum(h).start()

    @pl.loop(0, 8)
    def _(q):
        far_part(*chunk(q)).start()


    local[0].wait()
    local[1].wait()

    @pl.loop(0, TOK // 16)
    def _(i):
        rows = pl.ds(pl.multiple_of(i * 16, 16), 16)
        part = tok_v[rows, :].astype(F32)
        inverse = lax.rsqrt(jnp.sum(part * part, axis=1, keepdims=True) / D + epsilon)
        cot_own[rows, :] = (cot_v[rows, :].astype(F32) * inverse).astype(BF16)

    for i in (0, 1):
        cot_part(i).start()

    @pl.loop(8, 2 * CHUNKS)
    def _(q):
        far_part(*chunk(q)).start()

    @pl.loop(0, AHEAD)
    def _(q):
        near_part(*chunk(q)).start()

    local[2].wait()
    for h in range(HALVES):
        core_sum(h).wait_recv()

        @pl.loop(0, NX * NZH)
        def _(i):
            i, j = i // NZH, i % NZH
            pair_v[i, j, :, half(h)] = (
                frag_v[i, j, c, :, half(h)].astype(F32) + frag_r[i, j, :, half(h)].astype(F32)
            ).astype(BF16)

        for d in (2, 1, 3):
            x_sum(h, d).start()

    for i in (3, 4, 5, 6):
        local[i].wait()

    def s2(h):
        for d in (1, 3, 2):
            x_sum(h, d).wait_recv()

        @pl.loop(0, NZH)
        def _(j):
            total = pair_v[x, j, :, half(h)].astype(F32)
            for d in (1, 2, 3):
                total = total + xr[d - 1, j, :, half(h)].astype(F32)
            quad_v[j, :, half(h)] = total.astype(BF16)

        for d in (2, 1, 3):
            zh_sum(h, d).start()

    def s3(h):
        for d in (1, 3, 2):
            zh_sum(h, d).wait_recv()
        total = quad_v[zh, :, half(h)].astype(F32)
        for d in (1, 2, 3):
            total = total + zhr[d - 1, :, half(h)].astype(F32)
        picked = index_ref[0]
        chosen = gt_v[picked, :, half(h)]
        velocity = mt_v[picked, :, half(h)]
        delta = chosen - total / (NX * NZH * NC)
        new_velocity = outer_beta * velocity + delta
        new_params = chosen - outer_rate * (delta + outer_beta * new_velocity)
        params_v[x, zh, c, :, half(h)] = new_params.astype(BF16)
        for d in (2, 1, 3):
            zh_params(h, d).start()
        for i in range(4):
            ng_v[i, :, half(h)] = jnp.where(picked == i, new_params, gt_v[i, :, half(h)])
            nm_v[i, :, half(h)] = jnp.where(picked == i, new_velocity, mt_v[i, :, half(h)])

    def s4(h):
        for d in (1, 3, 2):
            zh_params(h, d).wait_recv()
        for d in (2, 1, 3):
            x_params(h, d).start()

    def s5(h):
        for d in (1, 3, 2):
            x_params(h, d).wait_recv()
        core_params(h).start()

    def s6(h):
        core_params(h).wait_recv()

        @pl.loop(0, NX * NZH)
        def _(i):
            i, j = i // NZH, i % NZH
            nf_v[i, j, :, :, half(h)] = (
                mix_weight * frag_v[i, j, :, :, half(h)].astype(F32)
                + (1.0 - mix_weight) * params_v[i, j, :, :, half(h)].astype(F32)
            ).astype(BF16)

    for i in (0, 1):
        cot_part(1 - i).wait_recv()

    def combine(q):
        o, b, k = chunk(q)
        far_part(o, b, k).wait_recv()
        part_s[at(b, k), :] = (
            dot_rows(tok_v[:, owned(NY - side(k), b, k)], cot_own[...])
            + dot_rows(far_v[:, at(b, k)], cot_near[k % 2])
        ).astype(BF16)
        product_part(o, b, k).start()

    def collect(o, b, k):
        near_part(o, b, k).wait_recv()
        mine = dot_rows(tok_v[:, owned(0, b, k)], cot_own[...]) + dot_rows(
            near_v[:, at(b, k)], cot_near[1 - k % 2]
        )
        product_part(o, b, k).wait_recv()
        return mine + part_v[at(b, k), :].astype(F32)

    def finish(q):
        o, _, k = chunk(q)
        rows = pl.ds(pl.multiple_of(k * WIDTH, WIDTH), WIDTH)

        @pl.when(o == 0)
        def _():
            zs[rows, :] = collect(o, 1 - zl, k).astype(BF16)
            z_part(k).start()

        @pl.when(o == 1)
        def _():
            mine = collect(o, zl, k)
            z_part(k).wait_recv()
            total = mine + zr[rows, :].astype(F32)
            where = pl.ds(pl.multiple_of(fs * BLOCK + k * WIDTH, WIDTH), WIDTH)
            terms = total * weight_v[rows, :].astype(F32)
            terms = sum(terms[:, i * 128 : (i + 1) * 128] for i in range(VW // 128))
            gg_v[:, where] = jnp.sum(terms.T, axis=0, keepdims=True)
            gains = jnp.broadcast_to(gain_v[:, where], (128, WIDTH)).T
            wg_v[rows, :] = (total * jnp.concatenate([gains] * (VW // 128), axis=1)).astype(BF16)

    steps = {
        0: [(s2, 0)],
        2: [(s2, 1)],
        3: [(s3, 0)],
        5: [(s3, 1)],
        6: [(s4, 0)],
        8: [(s4, 1)],
        10: [(s5, 0)],
        12: [(s5, 1)],
        14: [(s6, 0)],
        16: [(s6, 1)],
    }

    @pl.loop(0, 2 * CHUNKS + LAG)
    def _(q):
        @pl.when(q < 2 * CHUNKS)
        def _():
            combine(q)

            @pl.when(q + AHEAD < 2 * CHUNKS)
            def _():
                near_part(*chunk(q + AHEAD)).start()

        @pl.when(q >= LAG)
        def _():
            finish(q - LAG)

        for when, calls in steps.items():

            @pl.when(q == when)
            def _():
                for step, h in calls:
                    step(h)

    for i in (7, 3, 5, 4, 6, 2, 1):
        gain_part(i).start()

    for h in range(HALVES):
        core_sum(h).wait_send()
        core_params(h).wait_send()
        for d in (1, 2, 3):
            for part in (x_sum, zh_sum, zh_params, x_params):
                part(h, d).wait_send()
    for i in (0, 1):
        cot_part(i).wait_send()

    @pl.loop(0, CHUNKS)
    def _(k):
        for o in (0, 1):
            for part in (far_part, near_part, product_part):
                part(o, o, k).wait_send()
        z_part(k).wait_send()

    for i in range(1, 8):
        gain_part(i).wait_recv()
    for i in range(1, 8):
        gain_part(i).wait_send()


def store(*refs):
    copies = [pltpu.make_async_copy(refs[i], refs[5 + i], refs[10].at[i]) for i in range(5)]
    for copy in copies:
        copy.start()
    for copy in copies:
        copy.wait()


def body(tokens, cotangent, gain, value_weight, fragment, global_table, momentum_table, frag_index):
    grid = (NX, NZH, NC, ROWS, KVW)
    dma = pltpu.SemaphoreType.DMA
    any_space = pl.BlockSpec(memory_space=pl.ANY)
    results = (
        jax.ShapeDtypeStruct((BLOCK, VW), BF16),
        jax.ShapeDtypeStruct((1, D), F32),
        jax.ShapeDtypeStruct(grid, BF16),
        jax.ShapeDtypeStruct((4, ROWS, KVW), F32),
        jax.ShapeDtypeStruct((4, ROWS, KVW), F32),
    )
    found = pl.pallas_call(
        kernel,
        out_shape=[pltpu.VMEM(r.shape, r.dtype) for r in results],
        in_specs=[pl.BlockSpec(memory_space=pltpu.SMEM)] + [any_space] * 7,
        out_specs=[pl.BlockSpec(memory_space=pltpu.VMEM)] * 5,
        scratch_shapes=[
            pltpu.VMEM((TOK, D), BF16),
            pltpu.VMEM((TOK, 2 * BLOCK), BF16),
            pltpu.VMEM((TOK, 2 * BLOCK), BF16),
            pltpu.VMEM((2 * BLOCK, VW), BF16),
            pltpu.VMEM((2 * BLOCK, VW), BF16),
            pltpu.VMEM((TOK, VW), BF16),
            pltpu.VMEM((TOK, VW), BF16),
            pltpu.VMEM((2, TOK, VW), BF16),
            pltpu.VMEM((1, D), F32),
            pltpu.VMEM((BLOCK, VW), BF16),
            pltpu.VMEM((BLOCK, VW), BF16),
            pltpu.VMEM((BLOCK, VW), BF16),
            pltpu.VMEM(grid, BF16),
            pltpu.VMEM((NX, NZH, ROWS, KVW), BF16),
            pltpu.VMEM((NX, NZH, ROWS, KVW), BF16),
            pltpu.VMEM((NX - 1, NZH, ROWS, KVW), BF16),
            pltpu.VMEM((NZH, ROWS, KVW), BF16),
            pltpu.VMEM((NZH - 1, ROWS, KVW), BF16),
            pltpu.VMEM(grid, BF16),
        ]
        + [pltpu.VMEM((4, ROWS, KVW), F32)] * 2
        + [dma((7,))]
        + [dma((2, CHUNKS))] * 6
        + [dma((2,))] * 2
        + [dma((CHUNKS,))] * 2
        + [dma((7,))] * 2
        + [dma((HALVES,))] * 2
        + [dma((HALVES, 3))] * 8
        + [dma((HALVES,))] * 2,
        compiler_params=pltpu.CompilerParams(
            collective_id=0, has_side_effects=True, vmem_limit_bytes=56 << 20
        ),
        cost_estimate=pl.CostEstimate(
            flops=2 * 2 * TOK * D * VW, bytes_accessed=16 << 20, transcendentals=TOK
        ),
        name="round",
    )(
        frag_index.reshape(1),
        tokens,
        cotangent,
        gain,
        value_weight.reshape(BLOCK, VW),
        fragment.reshape(grid),
        global_table,
        momentum_table,
    )
    wg, gg, nf, ng, nm = pl.pallas_call(
        store,
        out_shape=results,
        in_specs=[any_space] * 5,
        out_specs=[any_space] * 5,
        scratch_shapes=[dma((5,))],
        compiler_params=pltpu.CompilerParams(vmem_limit_bytes=4 << 20),
        name="store",
    )(*found)
    return wg[None], gg, nf.reshape(1, BLOCK, KVW), ng, nm


def solution(mesh):
    placed = (
        P(("replica", "fsdp"), None),
        P(("replica", "fsdp"), None),
        P("replica", None),
        P("replica", "fsdp", None),
        P("replica", "fsdp", None),
        P(None, ("fsdp", "replica"), None),
        P(None, ("fsdp", "replica"), None),
        P(),
    )
    return jax.shard_map(
        body,
        mesh=mesh,
        in_specs=placed,
        out_specs=(
            P("replica", "fsdp", None),
            P("replica", None),
            P("replica", "fsdp", None),
            P(None, ("fsdp", "replica"), None),
            P(None, ("fsdp", "replica"), None),
        ),
        check_vma=False,
    )
```

```python
import functools

import jax
import jax.numpy as jnp
from jax import lax
from jax.experimental import pallas as pl
from jax.experimental.pallas import tpu as pltpu
from jax.sharding import PartitionSpec as P

MESH = pl.DeviceIdType.MESH
F32 = jnp.float32
BF16 = jnp.bfloat16

epsilon = 1e-05
outer_rate = 0.7
outer_beta = 0.9
mix_weight = 0.5

NX, NZH, NC = 4, 4, 2
NY, NZL = 4, 2
TOK = 256
D = 8192
BLOCK = 1024
VW = 512
KVW = 1024
ROWS = 32
CHUNKS = 8
WIDTH = BLOCK // CHUNKS
SPLIT = 6
DOWN = CHUNKS - SPLIT
AHEAD = 2
LAG = 4
HALVES = 4
HW = KVW // HALVES


def dot_rows(a, b):
    return lax.dot_general(a, b, (((0,), (0,)), ((), ())), preferred_element_type=F32)


def kernel(
    index_ref, tokens, cotangent, gain, weight, fragment, g_table, m_table,
    wg_v, gg_v, nf_v, ng_v, nm_v,
    tok_v, far_v, near_v, part_s, part_v, cot_v, cot_own, cot_near, gain_v,
    swap_v, cot_swap, away_s, away_v, side_s, side_v, sum_s, sum_v, weight_v, zs, zr,
    frag_v, frag_r, pair_v, xr, quad_v, zhr, params_v, gt_v, mt_v,
    lsem, far_s, far_r, near_s, near_r, part_ss, part_rs, cot_s, cot_r, z_s, z_r, gg_s, gg_r,
    swap_ss, swap_rs, cs_s, cs_r, away_ss, away_rs, side_ss, side_rs, sum_ss, sum_rs,
    fc_s, fc_r, xr_s, xr_r, zh_s, zh_r, az_s, az_r, ax_s, ax_r, ac_s, ac_r,
):
    rep = lax.axis_index("replica")
    fs = lax.axis_index("fsdp")
    x, zh, c = rep // (NZH * NC), (rep // NC) % NZH, rep % NC
    y, zl = fs // NZL, fs % NZL

    def device(dx=0, dzh=0, dc=0, dy=0, dz=0):
        return (
            (((x + dx) % NX) * NZH + (zh + dzh) % NZH) * NC + (c + dc) % NC,
            ((y + dy) % NY) * NZL + (zl + dz) % NZL,
        )

    def remote(src, dst, ssem, rsem, to):
        return pltpu.make_async_remote_copy(
            src_ref=src, dst_ref=dst, send_sem=ssem, recv_sem=rsem,
            device_id=to, device_id_type=MESH,
        )

    local = [
        pltpu.make_async_copy(src, dst, lsem.at[i])
        for i, (src, dst) in enumerate(
            (
                (tokens, tok_v),
                (cotangent, cot_v),
                (fragment, frag_v),
                (weight, weight_v),
                (gain, gain_v),
                (g_table, gt_v),
                (m_table, mt_v),
            )
        )
    ]
    for i in (2, 0, 1, 3, 4, 5, 6):
        local[i].start()

    near_partners = (
        [dict(dc=1)]
        + [dict(dx=d) for d in (1, 2, 3)]
        + [dict(dy=d) for d in (1, 2, 3)]
        + [dict(dz=1, dy=d) for d in range(4)]
    )
    barrier = pltpu.get_barrier_semaphore()

    def greet(to):
        pl.semaphore_signal(barrier, inc=1, device_id=to, device_id_type=MESH)

    for p in near_partners:
        greet(device(**p))

    @pl.when(zh >= 2)
    def _():
        greet(device(dzh=NZH + 5 - 2 * zh))
        pl.semaphore_wait(barrier, len(near_partners) + 3)
        greet(device(dzh=NZH - zh))
        greet(device(dzh=NZH + 1 - zh))

    @pl.when(zh < 2)
    def _():
        pl.semaphore_wait(barrier, len(near_partners) + zh)
        for d in (1, 2, 3):
            greet(device(dzh=d))

    def later_barrier():
        @pl.when(zh < 2)
        def _():
            pl.semaphore_wait(barrier, 3 - zh)

    def half(h):
        return pl.ds(h * HW, HW)

    def core_sum(h):
        return remote(
            fragment.at[:, :, 1 - c, :, half(h)], frag_r.at[:, :, :, half(h)],
            fc_s.at[h], fc_r.at[h], device(dc=1),
        )

    def x_sum(h, d):
        return remote(
            pair_v.at[(x + d) % NX, :, :, half(h)], xr.at[d - 1, :, :, half(h)],
            xr_s.at[h, d - 1], xr_r.at[h, d - 1], device(dx=d),
        )

    def zh_sum(h, d):
        return remote(
            quad_v.at[(zh + d) % NZH, :, half(h)], zhr.at[d - 1, :, half(h)],
            zh_s.at[h, d - 1], zh_r.at[h, d - 1], device(dzh=d),
        )

    def zh_params(h, d):
        part = params_v.at[x, zh, c, :, half(h)]
        return remote(part, part, az_s.at[h, d - 1], az_r.at[h, d - 1], device(dzh=d))

    def x_params(h, d):
        part = params_v.at[x, :, c, :, half(h)]
        return remote(part, part, ax_s.at[h, d - 1], ax_r.at[h, d - 1], device(dx=d))

    def core_params(h):
        part = params_v.at[:, :, c, :, half(h)]
        return remote(part, part, ac_s.at[h], ac_r.at[h], device(dc=1))

    def at(b, k):
        start = b * BLOCK + k * WIDTH
        return pl.ds(start if isinstance(start, int) else pl.multiple_of(start, WIDTH), WIDTH)

    def owned(d, b, k):
        return pl.ds(
            pl.multiple_of(((y + d) % NY) * 2 * BLOCK + b * BLOCK + k * WIDTH, WIDTH), WIDTH
        )

    def side(k):
        return 1 - 2 * (k % 2)

    def far_part(o, b, k):
        return remote(
            tokens.at[:, owned(2, b, k)], far_v.at[:, at(b, k)],
            far_s.at[o, k], far_r.at[o, k], device(dy=NY - side(k)),
        )

    def near_part(o, b, k):
        return remote(
            tokens.at[:, owned(NY + side(k), b, k)], near_v.at[:, at(b, k)],
            near_s.at[o, k], near_r.at[o, k], device(dy=NY + side(k)),
        )

    def product_part(o, b, k):
        return remote(
            part_s.at[at(b, k)], part_v.at[at(b, k)],
            part_ss.at[o, k], part_rs.at[o, k], device(dy=NY - side(k)),
        )

    def cot_part(i):
        return remote(
            cot_own, cot_near.at[1 - i], cot_s.at[i], cot_r.at[1 - i], device(dy=1 + 2 * i)
        )

    def swap_part(i, d):
        col = pl.multiple_of(d * 2 * BLOCK + (1 - zl) * BLOCK + (SPLIT + i) * WIDTH, WIDTH)
        return remote(
            tokens.at[:, pl.ds(col, WIDTH)], swap_v.at[i, d],
            swap_ss.at[i, d], swap_rs.at[i, d], device(dz=1),
        )

    def cot_swap_part():
        return remote(cot_own, cot_swap, cs_s, cs_r, device(dz=1))

    def away_part(i):
        return remote(
            away_s.at[i], away_v.at[i], away_ss.at[i], away_rs.at[i],
            device(dy=NY - side(SPLIT + i)),
        )

    def side_part(i):
        return remote(
            side_s.at[i], side_v.at[i], side_ss.at[i], side_rs.at[i],
            device(dy=NY + side(SPLIT + i)),
        )

    def sum_part(i):
        return remote(
            sum_s.at[i], sum_v.at[i], sum_ss.at[i], sum_rs.at[i],
            device(dy=NY - side(SPLIT + i)),
        )

    def chunk(q):
        first, last, odd = 1 - (q + 2 * SPLIT - 1) // (2 * SPLIT), (q + 1) // (2 * SPLIT), q % 2
        o = (1 - odd) * (1 - first) + last
        k = odd * ((q + 1) // 2 - last) + (1 - odd) * (q // 2 - 1 + first)
        return o, o * zl + (1 - o) * (1 - zl), k

    def z_part(k):
        rows = pl.ds(pl.multiple_of(k * WIDTH, WIDTH), WIDTH)
        return remote(zs.at[rows], zr.at[rows], z_s.at[k], z_r.at[k], device(dz=1))

    def gain_part(i):
        part = gg_v.at[:, pl.ds(pl.multiple_of(fs * BLOCK, BLOCK), BLOCK)]
        return remote(part, part, gg_s.at[i - 1], gg_r.at[i - 1], device(dy=i // 2, dz=i % 2))

    for h in range(HALVES):
        core_sum(h).start()

    @pl.loop(0, SPLIT)
    def _(q):
        far_part(*chunk(q)).start()

    for i in range(DOWN):
        for d in range(NY):
            swap_part(i, d).start()


    local[0].wait()
    local[1].wait()

    @pl.loop(0, TOK // 16)
    def _(i):
        rows = pl.ds(pl.multiple_of(i * 16, 16), 16)
        part = tok_v[rows, :].astype(F32)
        inverse = lax.rsqrt(jnp.sum(part * part, axis=1, keepdims=True) / D + epsilon)
        cot_own[rows, :] = (cot_v[rows, :].astype(F32) * inverse).astype(BF16)

    for i in (0, 1):
        cot_part(i).start()
    cot_swap_part().start()

    @pl.loop(SPLIT, 2 * SPLIT)
    def _(q):
        far_part(*chunk(q)).start()

    @pl.loop(0, AHEAD)
    def _(q):
        near_part(*chunk(q)).start()

    local[2].wait()
    for h in range(HALVES):
        core_sum(h).wait_recv()

        @pl.loop(0, NX * NZH)
        def _(i):
            i, j = i // NZH, i % NZH
            pair_v[i, j, :, half(h)] = (
                frag_v[i, j, c, :, half(h)].astype(F32) + frag_r[i, j, :, half(h)].astype(F32)
            ).astype(BF16)

        for d in (2, 1, 3):
            x_sum(h, d).start()

    for i in (3, 4, 5, 6):
        local[i].wait()

    def s2(h):
        for d in (1, 3, 2):
            x_sum(h, d).wait_recv()

        @pl.loop(0, NZH)
        def _(j):
            total = pair_v[x, j, :, half(h)].astype(F32)
            for d in (1, 2, 3):
                total = total + xr[d - 1, j, :, half(h)].astype(F32)
            quad_v[j, :, half(h)] = total.astype(BF16)

        if h == 0:
            later_barrier()
        for d in (2, 1, 3):
            zh_sum(h, d).start()

    def s3(h):
        for d in (1, 3, 2):
            zh_sum(h, d).wait_recv()
        total = quad_v[zh, :, half(h)].astype(F32)
        for d in (1, 2, 3):
            total = total + zhr[d - 1, :, half(h)].astype(F32)
        picked = index_ref[0]
        chosen = gt_v[picked, :, half(h)]
        velocity = mt_v[picked, :, half(h)]
        delta = chosen - total / (NX * NZH * NC)
        new_velocity = outer_beta * velocity + delta
        new_params = chosen - outer_rate * (delta + outer_beta * new_velocity)
        params_v[x, zh, c, :, half(h)] = new_params.astype(BF16)
        for d in (2, 1, 3):
            zh_params(h, d).start()
        for i in range(4):
            ng_v[i, :, half(h)] = jnp.where(picked == i, new_params, gt_v[i, :, half(h)])
            nm_v[i, :, half(h)] = jnp.where(picked == i, new_velocity, mt_v[i, :, half(h)])

    def s4(h):
        for d in (1, 3, 2):
            zh_params(h, d).wait_recv()
        for d in (2, 1, 3):
            x_params(h, d).start()

    def s5(h):
        for d in (1, 3, 2):
            x_params(h, d).wait_recv()
        core_params(h).start()

    def s6(h):
        core_params(h).wait_recv()

        @pl.loop(0, NX * NZH)
        def _(i):
            i, j = i // NZH, i % NZH
            nf_v[i, j, :, :, half(h)] = (
                mix_weight * frag_v[i, j, :, :, half(h)].astype(F32)
                + (1.0 - mix_weight) * params_v[i, j, :, :, half(h)].astype(F32)
            ).astype(BF16)

    for i in (0, 1):
        cot_part(1 - i).wait_recv()

    def combine(q):
        o, b, k = chunk(q)
        far_part(o, b, k).wait_recv()
        part_s[at(b, k), :] = (
            dot_rows(tok_v[:, owned(NY - side(k), b, k)], cot_own[...])
            + dot_rows(far_v[:, at(b, k)], cot_near[k % 2])
        ).astype(BF16)
        product_part(o, b, k).start()

    def collect(o, b, k):
        near_part(o, b, k).wait_recv()
        mine = dot_rows(tok_v[:, owned(0, b, k)], cot_own[...]) + dot_rows(
            near_v[:, at(b, k)], cot_near[1 - k % 2]
        )
        product_part(o, b, k).wait_recv()
        return mine + part_v[at(b, k), :].astype(F32)

    def conclude(k, total):
        rows = at(0, k)
        where = pl.ds(pl.multiple_of(fs * BLOCK + k * WIDTH, WIDTH), WIDTH)
        terms = total * weight_v[rows, :].astype(F32)
        terms = sum(terms[:, i * 128 : (i + 1) * 128] for i in range(VW // 128))
        gg_v[:, where] = jnp.sum(terms.T, axis=0, keepdims=True)
        gains = jnp.broadcast_to(gain_v[:, where], (128, WIDTH)).T
        wg_v[rows, :] = (total * jnp.concatenate([gains] * (VW // 128), axis=1)).astype(BF16)

    def finish(q):
        o, _, k = chunk(q)
        rows = pl.ds(pl.multiple_of(k * WIDTH, WIDTH), WIDTH)

        @pl.when(o == 0)
        def _():
            zs[rows, :] = collect(o, 1 - zl, k).astype(BF16)
            z_part(k).start()

        @pl.when(o == 1)
        def _():
            mine = collect(o, zl, k)
            z_part(k).wait_recv()
            conclude(k, mine + zr[rows, :].astype(F32))

    def both(i, d):
        if i == 0 and d == 2:
            cot_swap_part().wait_recv()
        if d == 2:
            for e in range(NY):
                swap_part(i, e).wait_recv()
        return dot_rows(tok_v[:, owned(d, zl, SPLIT + i)], cot_own[...]) + dot_rows(
            swap_v[i, (y + d) % NY], cot_swap[...]
        )

    def away(i):
        away_s[i] = both(i, 2).astype(BF16)
        away_part(i).start()

    def beside(i):
        side_s[i] = both(i, NY + side(SPLIT + i)).astype(BF16)
        side_part(i).start()

    def pass_on(i):
        mine = both(i, NY - side(SPLIT + i))
        away_part(i).wait_recv()
        sum_s[i] = (mine + away_v[i].astype(F32)).astype(BF16)
        sum_part(i).start()

    def add_up(i):
        mine = both(i, 0)
        side_part(i).wait_recv()
        sum_part(i).wait_recv()
        conclude(SPLIT + i, mine + side_v[i].astype(F32) + sum_v[i].astype(F32))

    steps = {
        0: [(away, 0)],
        1: [(s2, 0), (away, 1)],
        2: [(s2, 1), (beside, 0)],
        3: [(s3, 0), (s2, 2), (beside, 1)],
        4: [(s3, 1), (s2, 3), (pass_on, 0)],
        5: [(s3, 2), (pass_on, 1)],
        6: [(s4, 0), (s3, 3)],
        7: [(s4, 1), (add_up, 0)],
        8: [(s4, 2), (add_up, 1)],
        9: [(s5, 0), (s4, 3)],
        10: [(s5, 1)],
        11: [(s5, 2)],
        12: [(s6, 0), (s5, 3)],
        13: [(s6, 1)],
        14: [(s6, 2)],
        15: [(s6, 3)],
    }

    @pl.loop(0, 2 * SPLIT + LAG)
    def _(q):
        @pl.when(q < 2 * SPLIT)
        def _():
            combine(q)

            @pl.when(q + AHEAD < 2 * SPLIT)
            def _():
                near_part(*chunk(q + AHEAD)).start()

        @pl.when(q >= LAG)
        def _():
            finish(q - LAG)

        for when, calls in steps.items():

            @pl.when(q == when)
            def _():
                for step, h in calls:
                    step(h)

    for i in (7, 3, 5, 4, 6, 2, 1):
        gain_part(i).start()

    for h in range(HALVES):
        core_sum(h).wait_send()
        core_params(h).wait_send()
        for d in (1, 2, 3):
            for part in (x_sum, zh_sum, zh_params, x_params):
                part(h, d).wait_send()
    for i in (0, 1):
        cot_part(i).wait_send()

    cot_swap_part().wait_send()
    for i in range(DOWN):
        for d in range(NY):
            swap_part(i, d).wait_send()
        for part in (away_part, side_part, sum_part):
            part(i).wait_send()

    @pl.loop(0, SPLIT)
    def _(k):
        for o in (0, 1):
            for part in (far_part, near_part, product_part):
                part(o, o, k).wait_send()
        z_part(k).wait_send()

    for i in range(1, 8):
        gain_part(i).wait_recv()
    for i in range(1, 8):
        gain_part(i).wait_send()


def store(*refs):
    copies = [pltpu.make_async_copy(refs[i], refs[5 + i], refs[10].at[i]) for i in range(5)]
    for copy in copies:
        copy.start()
    for copy in copies:
        copy.wait()


def body(tokens, cotangent, gain, value_weight, fragment, global_table, momentum_table, frag_index):
    grid = (NX, NZH, NC, ROWS, KVW)
    dma = pltpu.SemaphoreType.DMA
    any_space = pl.BlockSpec(memory_space=pl.ANY)
    results = (
        jax.ShapeDtypeStruct((BLOCK, VW), BF16),
        jax.ShapeDtypeStruct((1, D), F32),
        jax.ShapeDtypeStruct(grid, BF16),
        jax.ShapeDtypeStruct((4, ROWS, KVW), F32),
        jax.ShapeDtypeStruct((4, ROWS, KVW), F32),
    )
    found = pl.pallas_call(
        kernel,
        out_shape=[pltpu.VMEM(r.shape, r.dtype) for r in results],
        in_specs=[pl.BlockSpec(memory_space=pltpu.SMEM)] + [any_space] * 7,
        out_specs=[pl.BlockSpec(memory_space=pltpu.VMEM)] * 5,
        scratch_shapes=[
            pltpu.VMEM((TOK, D), BF16),
            pltpu.VMEM((TOK, 2 * BLOCK), BF16),
            pltpu.VMEM((TOK, 2 * BLOCK), BF16),
            pltpu.VMEM((2 * BLOCK, VW), BF16),
            pltpu.VMEM((2 * BLOCK, VW), BF16),
            pltpu.VMEM((TOK, VW), BF16),
            pltpu.VMEM((TOK, VW), BF16),
            pltpu.VMEM((2, TOK, VW), BF16),
            pltpu.VMEM((1, D), F32),
            pltpu.VMEM((DOWN, NY, TOK, WIDTH), BF16),
            pltpu.VMEM((TOK, VW), BF16),
        ]
        + [pltpu.VMEM((DOWN, WIDTH, VW), BF16)] * 6
        + [
            pltpu.VMEM((BLOCK, VW), BF16),
            pltpu.VMEM((BLOCK, VW), BF16),
            pltpu.VMEM((BLOCK, VW), BF16),
            pltpu.VMEM(grid, BF16),
            pltpu.VMEM((NX, NZH, ROWS, KVW), BF16),
            pltpu.VMEM((NX, NZH, ROWS, KVW), BF16),
            pltpu.VMEM((NX - 1, NZH, ROWS, KVW), BF16),
            pltpu.VMEM((NZH, ROWS, KVW), BF16),
            pltpu.VMEM((NZH - 1, ROWS, KVW), BF16),
            pltpu.VMEM(grid, BF16),
        ]
        + [pltpu.VMEM((4, ROWS, KVW), F32)] * 2
        + [dma((7,))]
        + [dma((2, CHUNKS))] * 6
        + [dma((2,))] * 2
        + [dma((CHUNKS,))] * 2
        + [dma((7,))] * 2
        + [dma((DOWN, NY))] * 2
        + [dma] * 2
        + [dma((DOWN,))] * 6
        + [dma((HALVES,))] * 2
        + [dma((HALVES, 3))] * 8
        + [dma((HALVES,))] * 2,
        compiler_params=pltpu.CompilerParams(
            collective_id=0, has_side_effects=True, vmem_limit_bytes=56 << 20
        ),
        cost_estimate=pl.CostEstimate(
            flops=2 * 2 * TOK * D * VW, bytes_accessed=16 << 20, transcendentals=TOK
        ),
        name="round",
    )(
        frag_index.reshape(1),
        tokens,
        cotangent,
        gain,
        value_weight.reshape(BLOCK, VW),
        fragment.reshape(grid),
        global_table,
        momentum_table,
    )
    wg, gg, nf, ng, nm = pl.pallas_call(
        store,
        out_shape=results,
        in_specs=[any_space] * 5,
        out_specs=[any_space] * 5,
        scratch_shapes=[dma((5,))],
        compiler_params=pltpu.CompilerParams(vmem_limit_bytes=4 << 20),
        name="store",
    )(*found)
    return wg[None], gg, nf.reshape(1, BLOCK, KVW), ng, nm


def solution(mesh):
    placed = (
        P(("replica", "fsdp"), None),
        P(("replica", "fsdp"), None),
        P("replica", None),
        P("replica", "fsdp", None),
        P("replica", "fsdp", None),
        P(None, ("fsdp", "replica"), None),
        P(None, ("fsdp", "replica"), None),
        P(),
    )
    return jax.shard_map(
        body,
        mesh=mesh,
        in_specs=placed,
        out_specs=(
            P("replica", "fsdp", None),
            P("replica", None),
            P("replica", "fsdp", None),
            P(None, ("fsdp", "replica"), None),
            P(None, ("fsdp", "replica"), None),
        ),
        check_vma=False,
    )
```

```python
import functools

import jax
import jax.numpy as jnp
from jax import lax
from jax.experimental import pallas as pl
from jax.experimental.pallas import tpu as pltpu
from jax.sharding import PartitionSpec as P

MESH = pl.DeviceIdType.MESH
F32 = jnp.float32
BF16 = jnp.bfloat16

epsilon = 1e-05
outer_rate = 0.7
outer_beta = 0.9
mix_weight = 0.5

NX, NZH, NC = 4, 4, 2
NY, NZL = 4, 2
TOK = 256
D = 8192
BLOCK = 1024
VW = 512
KVW = 1024
ROWS = 32
CHUNKS = 8
WIDTH = BLOCK // CHUNKS
SPLIT = 6
DOWN = CHUNKS - SPLIT
AHEAD = 3
LAG = 4
HALVES = 4
HW = KVW // HALVES


def dot_rows(a, b):
    return lax.dot_general(a, b, (((0,), (0,)), ((), ())), preferred_element_type=F32)


def kernel(
    index_ref, tokens, cotangent, gain, weight, fragment, g_table, m_table,
    wg_v, gg_v, nf_v, ng_v, nm_v,
    tok_v, far_v, near_v, part_s, part_v, cot_v, cot_own, cot_near, gain_v,
    swap_v, cot_swap, away_s, away_v, side_s, side_v, sum_s, sum_v, weight_v, zs, zr,
    frag_v, frag_r, pair_v, xr, quad_v, zhr, params_v, gt_v, mt_v,
    lsem, far_s, far_r, near_s, near_r, part_ss, part_rs, cot_s, cot_r, z_s, z_r, gg_s, gg_r,
    swap_ss, swap_rs, cs_s, cs_r, away_ss, away_rs, side_ss, side_rs, sum_ss, sum_rs,
    fc_s, fc_r, xr_s, xr_r, zh_s, zh_r, az_s, az_r, ax_s, ax_r, ac_s, ac_r,
):
    rep = lax.axis_index("replica")
    fs = lax.axis_index("fsdp")
    x, zh, c = rep // (NZH * NC), (rep // NC) % NZH, rep % NC
    y, zl = fs // NZL, fs % NZL

    def device(dx=0, dzh=0, dc=0, dy=0, dz=0):
        return (
            (((x + dx) % NX) * NZH + (zh + dzh) % NZH) * NC + (c + dc) % NC,
            ((y + dy) % NY) * NZL + (zl + dz) % NZL,
        )

    def remote(src, dst, ssem, rsem, to):
        return pltpu.make_async_remote_copy(
            src_ref=src, dst_ref=dst, send_sem=ssem, recv_sem=rsem,
            device_id=to, device_id_type=MESH,
        )

    local = [
        pltpu.make_async_copy(src, dst, lsem.at[i])
        for i, (src, dst) in enumerate(
            (
                (tokens, tok_v),
                (cotangent, cot_v),
                (fragment, frag_v),
                (weight, weight_v),
                (gain, gain_v),
                (g_table, gt_v),
                (m_table, mt_v),
            )
        )
    ]

    near_partners = (
        [dict(dc=1)]
        + [dict(dx=d) for d in (1, 2, 3)]
        + [dict(dy=d) for d in (1, 2, 3)]
        + [dict(dz=1, dy=d) for d in range(4)]
    )
    barrier = pltpu.get_barrier_semaphore()

    def greet(to):
        pl.semaphore_signal(barrier, inc=1, device_id=to, device_id_type=MESH)

    for p in near_partners:
        greet(device(**p))

    for i in (0, 1, 2, 3, 4, 5, 6):
        local[i].start()

    @pl.when(zh >= 2)
    def _():
        greet(device(dzh=NZH + 5 - 2 * zh))
        pl.semaphore_wait(barrier, len(near_partners) + 3)
        greet(device(dzh=NZH - zh))
        greet(device(dzh=NZH + 1 - zh))

    @pl.when(zh < 2)
    def _():
        pl.semaphore_wait(barrier, len(near_partners) + zh)
        for d in (1, 2, 3):
            greet(device(dzh=d))

    def later_barrier():
        @pl.when(zh < 2)
        def _():
            pl.semaphore_wait(barrier, 3 - zh)

    def half(h):
        return pl.ds(h * HW, HW)

    def core_sum(h):
        return remote(
            fragment.at[:, :, 1 - c, :, half(h)], frag_r.at[:, :, :, half(h)],
            fc_s.at[h], fc_r.at[h], device(dc=1),
        )

    def x_sum(h, d):
        return remote(
            pair_v.at[(x + d) % NX, :, :, half(h)], xr.at[d - 1, :, :, half(h)],
            xr_s.at[h, d - 1], xr_r.at[h, d - 1], device(dx=d),
        )

    def zh_sum(h, d):
        return remote(
            quad_v.at[(zh + d) % NZH, :, half(h)], zhr.at[d - 1, :, half(h)],
            zh_s.at[h, d - 1], zh_r.at[h, d - 1], device(dzh=d),
        )

    def zh_params(h, d):
        part = params_v.at[x, zh, c, :, half(h)]
        return remote(part, part, az_s.at[h, d - 1], az_r.at[h, d - 1], device(dzh=d))

    def x_params(h, d):
        part = params_v.at[x, :, c, :, half(h)]
        return remote(part, part, ax_s.at[h, d - 1], ax_r.at[h, d - 1], device(dx=d))

    def core_params(h):
        part = params_v.at[:, :, c, :, half(h)]
        return remote(part, part, ac_s.at[h], ac_r.at[h], device(dc=1))

    def at(b, k):
        start = b * BLOCK + k * WIDTH
        return pl.ds(start if isinstance(start, int) else pl.multiple_of(start, WIDTH), WIDTH)

    def owned(d, b, k):
        return pl.ds(
            pl.multiple_of(((y + d) % NY) * 2 * BLOCK + b * BLOCK + k * WIDTH, WIDTH), WIDTH
        )

    def turn(o, k):
        return (1 - o) * ((k + SPLIT - 1) // SPLIT) + o * ((k + 1) // SPLIT)

    def side(o, k):
        return 1 - 2 * turn(o, k)

    def far_part(o, b, k):
        return remote(
            tokens.at[:, owned(2, b, k)], far_v.at[:, at(b, k)],
            far_s.at[o, k], far_r.at[o, k], device(dy=NY - side(o, k)),
        )

    def near_part(o, b, k):
        return remote(
            tokens.at[:, owned(NY + side(o, k), b, k)], near_v.at[:, at(b, k)],
            near_s.at[o, k], near_r.at[o, k], device(dy=NY + side(o, k)),
        )

    def product_part(o, b, k):
        return remote(
            part_s.at[at(b, k)], part_v.at[at(b, k)],
            part_ss.at[o, k], part_rs.at[o, k], device(dy=NY - side(o, k)),
        )

    def cot_part(i):
        return remote(
            cot_own, cot_near.at[1 - i], cot_s.at[i], cot_r.at[1 - i], device(dy=1 + 2 * i)
        )

    def swap_part(i, d):
        col = pl.multiple_of(d * 2 * BLOCK + (1 - zl) * BLOCK + (SPLIT + i) * WIDTH, WIDTH)
        return remote(
            tokens.at[:, pl.ds(col, WIDTH)], swap_v.at[i, d],
            swap_ss.at[i, d], swap_rs.at[i, d], device(dz=1),
        )

    def cot_swap_part():
        return remote(cot_own, cot_swap, cs_s, cs_r, device(dz=1))

    def away_part(i):
        return remote(
            away_s.at[i], away_v.at[i], away_ss.at[i], away_rs.at[i],
            device(dy=NY - 1 + 2 * (i % 2)),
        )

    def side_part(i):
        return remote(
            side_s.at[i], side_v.at[i], side_ss.at[i], side_rs.at[i],
            device(dy=NY + 1 - 2 * (i % 2)),
        )

    def sum_part(i):
        return remote(
            sum_s.at[i], sum_v.at[i], sum_ss.at[i], sum_rs.at[i],
            device(dy=NY - 1 + 2 * (i % 2)),
        )

    def chunk(q):
        first, last, odd = 1 - (q + 2 * SPLIT - 1) // (2 * SPLIT), (q + 1) // (2 * SPLIT), q % 2
        o = (1 - odd) * (1 - first) + last
        k = odd * ((q + 1) // 2 - last) + (1 - odd) * (q // 2 - 1 + first)
        return o, o * zl + (1 - o) * (1 - zl), k

    def z_part(k):
        rows = pl.ds(pl.multiple_of(k * WIDTH, WIDTH), WIDTH)
        return remote(zs.at[rows], zr.at[rows], z_s.at[k], z_r.at[k], device(dz=1))

    def gain_part(i):
        part = gg_v.at[:, pl.ds(pl.multiple_of(fs * BLOCK, BLOCK), BLOCK)]
        return remote(part, part, gg_s.at[i - 1], gg_r.at[i - 1], device(dy=i // 2, dz=i % 2))


    @pl.loop(0, SPLIT)
    def _(q):
        far_part(*chunk(q)).start()

    for h in range(HALVES):
        core_sum(h).start()
    for i in range(DOWN):
        for d in range(NY):
            swap_part(i, d).start()


    local[0].wait()
    local[1].wait()

    @pl.loop(0, TOK // 16)
    def _(i):
        rows = pl.ds(pl.multiple_of(i * 16, 16), 16)
        part = tok_v[rows, :].astype(F32)
        inverse = lax.rsqrt(jnp.sum(part * part, axis=1, keepdims=True) / D + epsilon)
        cot_own[rows, :] = (cot_v[rows, :].astype(F32) * inverse).astype(BF16)

    for i in (0, 1):
        cot_part(i).start()
    cot_swap_part().start()

    @pl.loop(SPLIT, 2 * SPLIT)
    def _(q):
        far_part(*chunk(q)).start()

    @pl.loop(0, AHEAD)
    def _(q):
        near_part(*chunk(q)).start()

    local[2].wait()
    for h in range(HALVES):
        core_sum(h).wait_recv()

        @pl.loop(0, NX * NZH)
        def _(i):
            i, j = i // NZH, i % NZH
            pair_v[i, j, :, half(h)] = (
                frag_v[i, j, c, :, half(h)].astype(F32) + frag_r[i, j, :, half(h)].astype(F32)
            ).astype(BF16)

        for d in (2, 1, 3):
            x_sum(h, d).start()

    for i in (3, 4, 5, 6):
        local[i].wait()

    def s2(h):
        for d in (1, 3, 2):
            x_sum(h, d).wait_recv()

        @pl.loop(0, NZH)
        def _(j):
            total = pair_v[x, j, :, half(h)].astype(F32)
            for d in (1, 2, 3):
                total = total + xr[d - 1, j, :, half(h)].astype(F32)
            quad_v[j, :, half(h)] = total.astype(BF16)

        if h == 0:
            later_barrier()
        for d in (2, 1, 3):
            zh_sum(h, d).start()

    def s3(h):
        for d in (1, 3, 2):
            zh_sum(h, d).wait_recv()
        total = quad_v[zh, :, half(h)].astype(F32)
        for d in (1, 2, 3):
            total = total + zhr[d - 1, :, half(h)].astype(F32)
        picked = index_ref[0]
        chosen = gt_v[picked, :, half(h)]
        velocity = mt_v[picked, :, half(h)]
        delta = chosen - total / (NX * NZH * NC)
        new_velocity = outer_beta * velocity + delta
        new_params = chosen - outer_rate * (delta + outer_beta * new_velocity)
        params_v[x, zh, c, :, half(h)] = new_params.astype(BF16)
        for d in (2, 1, 3):
            zh_params(h, d).start()
        for i in range(4):
            ng_v[i, :, half(h)] = jnp.where(picked == i, new_params, gt_v[i, :, half(h)])
            nm_v[i, :, half(h)] = jnp.where(picked == i, new_velocity, mt_v[i, :, half(h)])

    def s4(h):
        for d in (1, 3, 2):
            zh_params(h, d).wait_recv()
        for d in (2, 1, 3):
            x_params(h, d).start()

    def s5(h):
        for d in (1, 3, 2):
            x_params(h, d).wait_recv()
        core_params(h).start()

    def s6(h):
        core_params(h).wait_recv()
        core_sum(h).wait_send()
        for d in (1, 2, 3):
            for part in (x_sum, zh_sum, zh_params, x_params):
                part(h, d).wait_send()
        if h > 0:
            core_params(h - 1).wait_send()

        @pl.loop(0, NX * NZH)
        def _(i):
            i, j = i // NZH, i % NZH
            nf_v[i, j, :, :, half(h)] = (
                mix_weight * frag_v[i, j, :, :, half(h)].astype(F32)
                + (1.0 - mix_weight) * params_v[i, j, :, :, half(h)].astype(F32)
            ).astype(BF16)

    for i in (0, 1):
        cot_part(1 - i).wait_recv()

    def combine(q):
        o, b, k = chunk(q)
        far_part(o, b, k).wait_recv()
        part_s[at(b, k), :] = (
            dot_rows(tok_v[:, owned(NY - side(o, k), b, k)], cot_own[...])
            + dot_rows(far_v[:, at(b, k)], cot_near[turn(o, k)])
        ).astype(BF16)
        product_part(o, b, k).start()

    def collect(o, b, k):
        near_part(o, b, k).wait_recv()
        mine = dot_rows(tok_v[:, owned(0, b, k)], cot_own[...]) + dot_rows(
            near_v[:, at(b, k)], cot_near[1 - turn(o, k)]
        )
        product_part(o, b, k).wait_recv()
        return mine + part_v[at(b, k), :].astype(F32)

    def conclude(k, total):
        rows = at(0, k)
        where = pl.ds(pl.multiple_of(fs * BLOCK + k * WIDTH, WIDTH), WIDTH)
        terms = total * weight_v[rows, :].astype(F32)
        terms = sum(terms[:, i * 128 : (i + 1) * 128] for i in range(VW // 128))
        gg_v[:, where] = jnp.sum(terms.T, axis=0, keepdims=True)
        gains = jnp.broadcast_to(gain_v[:, where], (128, WIDTH)).T
        wg_v[rows, :] = (total * jnp.concatenate([gains] * (VW // 128), axis=1)).astype(BF16)

    def sent(q):
        o, b, k = chunk(q)
        for part in (far_part, near_part, product_part):
            part(o, b, k).wait_send()

    def finish(q):
        o, _, k = chunk(q)
        rows = pl.ds(pl.multiple_of(k * WIDTH, WIDTH), WIDTH)

        @pl.when(o == 0)
        def _():
            zs[rows, :] = collect(o, 1 - zl, k).astype(BF16)
            z_part(k).start()

        @pl.when(o == 1)
        def _():
            mine = collect(o, zl, k)
            z_part(k).wait_recv()
            conclude(k, mine + zr[rows, :].astype(F32))

    def both(i, d):
        if i == 0 and d == 2:
            cot_swap_part().wait_recv()
        if d == 2:
            for e in range(NY):
                swap_part(i, e).wait_recv()
        return dot_rows(tok_v[:, owned(d, zl, SPLIT + i)], cot_own[...]) + dot_rows(
            swap_v[i, (y + d) % NY], cot_swap[...]
        )

    def away(i):
        away_s[i] = both(i, 2).astype(BF16)
        away_part(i).start()

    def beside(i):
        side_s[i] = both(i, NY + 1 - 2 * (i % 2)).astype(BF16)
        side_part(i).start()

    def pass_on(i):
        mine = both(i, NY - 1 + 2 * (i % 2))
        away_part(i).wait_recv()
        sum_s[i] = (mine + away_v[i].astype(F32)).astype(BF16)
        sum_part(i).start()

    def add_up(i):
        if i == 0:
            for j in (0, 1):
                cot_part(j).wait_send()
            cot_swap_part().wait_send()
        for d in range(NY):
            swap_part(i, d).wait_send()
        for part in (away_part, side_part):
            part(i).wait_send()
        mine = both(i, 0)
        side_part(i).wait_recv()
        sum_part(i).wait_recv()
        conclude(SPLIT + i, mine + side_v[i].astype(F32) + sum_v[i].astype(F32))

    steps = {
        1: [(s2, 0)],
        2: [(away, 0), (s2, 1)],
        3: [(s2, 2)],
        4: [(s3, 0), (away, 1), (s2, 3)],
        5: [(s3, 1), (beside, 0)],
        6: [(s3, 2), (pass_on, 0)],
        7: [(s4, 0), (s3, 3), (beside, 1)],
        8: [(s4, 1), (pass_on, 1)],
        9: [(s4, 2)],
        10: [(s4, 3), (add_up, 0)],
        11: [(s5, 0), (s5, 1), (add_up, 1)],
        12: [(s5, 2)],
        13: [(s5, 3)],
        14: [(s6, 0), (s6, 1)],
        15: [(s6, 2), (s6, 3)],
    }

    @pl.loop(0, 2 * SPLIT + LAG)
    def _(q):
        @pl.when(q < 2 * SPLIT)
        def _():
            combine(q)

            @pl.when(q + AHEAD < 2 * SPLIT)
            def _():
                near_part(*chunk(q + AHEAD)).start()

        for when, calls in steps.items():

            @pl.when(q == when)
            def _():
                for step, h in calls:
                    step(h)

        @pl.when(q >= LAG)
        def _():
            finish(q - LAG)

        @pl.when((q >= LAG) & (q < 2 * SPLIT))
        def _():
            sent(q - LAG)

    for i in (7, 3, 5, 4, 6, 2, 1):
        gain_part(i).start()

    core_params(HALVES - 1).wait_send()
    for i in range(DOWN):
        sum_part(i).wait_send()

    @pl.loop(2 * SPLIT - LAG, 2 * SPLIT)
    def _(q):
        sent(q)

    for k in range(SPLIT):
        z_part(k).wait_send()

    for i in range(1, 8):
        gain_part(i).wait_recv()
    for i in range(1, 8):
        gain_part(i).wait_send()


def store(*refs):
    copies = [pltpu.make_async_copy(refs[i], refs[5 + i], refs[10].at[i]) for i in range(5)]
    for copy in copies:
        copy.start()
    for copy in copies:
        copy.wait()


def body(tokens, cotangent, gain, value_weight, fragment, global_table, momentum_table, frag_index):
    grid = (NX, NZH, NC, ROWS, KVW)
    dma = pltpu.SemaphoreType.DMA
    any_space = pl.BlockSpec(memory_space=pl.ANY)
    results = (
        jax.ShapeDtypeStruct((BLOCK, VW), BF16),
        jax.ShapeDtypeStruct((1, D), F32),
        jax.ShapeDtypeStruct(grid, BF16),
        jax.ShapeDtypeStruct((4, ROWS, KVW), F32),
        jax.ShapeDtypeStruct((4, ROWS, KVW), F32),
    )
    found = pl.pallas_call(
        kernel,
        out_shape=[pltpu.VMEM(r.shape, r.dtype) for r in results],
        in_specs=[pl.BlockSpec(memory_space=pltpu.SMEM)] + [any_space] * 7,
        out_specs=[pl.BlockSpec(memory_space=pltpu.VMEM)] * 5,
        scratch_shapes=[
            pltpu.VMEM((TOK, D), BF16),
            pltpu.VMEM((TOK, 2 * BLOCK), BF16),
            pltpu.VMEM((TOK, 2 * BLOCK), BF16),
            pltpu.VMEM((2 * BLOCK, VW), BF16),
            pltpu.VMEM((2 * BLOCK, VW), BF16),
            pltpu.VMEM((TOK, VW), BF16),
            pltpu.VMEM((TOK, VW), BF16),
            pltpu.VMEM((2, TOK, VW), BF16),
            pltpu.VMEM((1, D), F32),
            pltpu.VMEM((DOWN, NY, TOK, WIDTH), BF16),
            pltpu.VMEM((TOK, VW), BF16),
        ]
        + [pltpu.VMEM((DOWN, WIDTH, VW), BF16)] * 6
        + [
            pltpu.VMEM((BLOCK, VW), BF16),
            pltpu.VMEM((BLOCK, VW), BF16),
            pltpu.VMEM((BLOCK, VW), BF16),
            pltpu.VMEM(grid, BF16),
            pltpu.VMEM((NX, NZH, ROWS, KVW), BF16),
            pltpu.VMEM((NX, NZH, ROWS, KVW), BF16),
            pltpu.VMEM((NX - 1, NZH, ROWS, KVW), BF16),
            pltpu.VMEM((NZH, ROWS, KVW), BF16),
            pltpu.VMEM((NZH - 1, ROWS, KVW), BF16),
            pltpu.VMEM(grid, BF16),
        ]
        + [pltpu.VMEM((4, ROWS, KVW), F32)] * 2
        + [dma((7,))]
        + [dma((2, CHUNKS))] * 6
        + [dma((2,))] * 2
        + [dma((CHUNKS,))] * 2
        + [dma((7,))] * 2
        + [dma((DOWN, NY))] * 2
        + [dma] * 2
        + [dma((DOWN,))] * 6
        + [dma((HALVES,))] * 2
        + [dma((HALVES, 3))] * 8
        + [dma((HALVES,))] * 2,
        compiler_params=pltpu.CompilerParams(
            collective_id=0, has_side_effects=True, vmem_limit_bytes=56 << 20
        ),
        cost_estimate=pl.CostEstimate(
            flops=2 * 2 * TOK * D * VW, bytes_accessed=16 << 20, transcendentals=TOK
        ),
        name="round",
    )(
        frag_index.reshape(1),
        tokens,
        cotangent,
        gain,
        value_weight.reshape(BLOCK, VW),
        fragment.reshape(grid),
        global_table,
        momentum_table,
    )
    wg, gg, nf, ng, nm = pl.pallas_call(
        store,
        out_shape=results,
        in_specs=[any_space] * 5,
        out_specs=[any_space] * 5,
        scratch_shapes=[dma((5,))],
        compiler_params=pltpu.CompilerParams(vmem_limit_bytes=4 << 20),
        name="store",
    )(*found)
    return wg[None], gg, nf.reshape(1, BLOCK, KVW), ng, nm


def solution(mesh):
    placed = (
        P(("replica", "fsdp"), None),
        P(("replica", "fsdp"), None),
        P("replica", None),
        P("replica", "fsdp", None),
        P("replica", "fsdp", None),
        P(None, ("fsdp", "replica"), None),
        P(None, ("fsdp", "replica"), None),
        P(),
    )
    return jax.shard_map(
        body,
        mesh=mesh,
        in_specs=placed,
        out_specs=(
            P("replica", "fsdp", None),
            P("replica", None),
            P("replica", "fsdp", None),
            P(None, ("fsdp", "replica"), None),
            P(None, ("fsdp", "replica"), None),
        ),
        check_vma=False,
    )
```

```python
import functools

import jax
import jax.numpy as jnp
from jax import lax
from jax.experimental import pallas as pl
from jax.experimental.pallas import tpu as pltpu
from jax.sharding import PartitionSpec as P

MESH = pl.DeviceIdType.MESH
F32 = jnp.float32
BF16 = jnp.bfloat16

epsilon = 1e-05
outer_rate = 0.7
outer_beta = 0.9
mix_weight = 0.5

NX, NZH, NC = 4, 4, 2
NY, NZL = 4, 2
TOK = 256
D = 8192
BLOCK = 1024
VW = 512
KVW = 1024
ROWS = 32
CHUNKS = 8
WIDTH = BLOCK // CHUNKS
SPLIT = 6
DOWN = CHUNKS - SPLIT
AHEAD = 3
LAG = 4
HALVES = 4
HW = KVW // HALVES


def dot_rows(a, b):
    return lax.dot_general(a, b, (((0,), (0,)), ((), ())), preferred_element_type=F32)


def kernel(
    index_ref, tokens, cotangent, gain, weight, fragment, g_table, m_table,
    wg_v, gg_v, nf_v, ng_v, nm_v,
    tok_v, far_v, near_v, part_s, part_v, cot_v, cot_own, cot_near, gain_v,
    swap_v, cot_swap, away_s, away_v, side_s, side_v, sum_s, sum_v, weight_v, zs, zr,
    frag_v, frag_r, pair_v, xr, quad_v, zhr, params_v, gt_v, mt_v,
    lsem, far_s, far_r, near_s, near_r, part_ss, part_rs, cot_s, cot_r, z_s, z_r, gg_s, gg_r,
    swap_ss, swap_rs, cs_s, cs_r, away_ss, away_rs, side_ss, side_rs, sum_ss, sum_rs,
    fc_s, fc_r, xr_s, xr_r, zh_s, zh_r, az_s, az_r, ax_s, ax_r, ac_s, ac_r,
):
    rep = lax.axis_index("replica")
    fs = lax.axis_index("fsdp")
    x, zh, c = rep // (NZH * NC), (rep // NC) % NZH, rep % NC
    y, zl = fs // NZL, fs % NZL

    def device(dx=0, dzh=0, dc=0, dy=0, dz=0):
        return (
            (((x + dx) % NX) * NZH + (zh + dzh) % NZH) * NC + (c + dc) % NC,
            ((y + dy) % NY) * NZL + (zl + dz) % NZL,
        )

    def remote(src, dst, ssem, rsem, to):
        return pltpu.make_async_remote_copy(
            src_ref=src, dst_ref=dst, send_sem=ssem, recv_sem=rsem,
            device_id=to, device_id_type=MESH,
        )

    local = [
        pltpu.make_async_copy(src, dst, lsem.at[i])
        for i, (src, dst) in enumerate(
            (
                (tokens, tok_v),
                (cotangent, cot_v),
                (fragment, frag_v),
                (weight, weight_v),
                (gain, gain_v),
                (g_table, gt_v),
                (m_table, mt_v),
            )
        )
    ]

    near_partners = (
        [dict(dc=1)]
        + [dict(dx=d) for d in (1, 2, 3)]
        + [dict(dy=d) for d in (1, 2, 3)]
        + [dict(dz=1, dy=d) for d in range(4)]
    )
    barrier = pltpu.get_barrier_semaphore()

    def greet(to):
        pl.semaphore_signal(barrier, inc=1, device_id=to, device_id_type=MESH)

    for p in near_partners:
        greet(device(**p))

    for i in (0, 1, 2, 3, 4, 5, 6):
        local[i].start()

    @pl.when(zh >= 2)
    def _():
        greet(device(dzh=NZH + 5 - 2 * zh))
        pl.semaphore_wait(barrier, len(near_partners) + 3)
        greet(device(dzh=NZH - zh))
        greet(device(dzh=NZH + 1 - zh))

    @pl.when(zh < 2)
    def _():
        pl.semaphore_wait(barrier, len(near_partners) + zh)
        for d in (1, 2, 3):
            greet(device(dzh=d))

    def later_barrier():
        @pl.when(zh < 2)
        def _():
            pl.semaphore_wait(barrier, 3 - zh)

    def half(h):
        return pl.ds(h * HW, HW)

    def core_sum(h):
        return remote(
            fragment.at[:, :, 1 - c, :, half(h)], frag_r.at[:, :, :, half(h)],
            fc_s.at[h], fc_r.at[h], device(dc=1),
        )

    def x_sum(h, d):
        return remote(
            pair_v.at[(x + d) % NX, :, :, half(h)], xr.at[d - 1, :, :, half(h)],
            xr_s.at[h, d - 1], xr_r.at[h, d - 1], device(dx=d),
        )

    def zh_sum(h, d):
        return remote(
            quad_v.at[(zh + d) % NZH, :, half(h)], zhr.at[d - 1, :, half(h)],
            zh_s.at[h, d - 1], zh_r.at[h, d - 1], device(dzh=d),
        )

    def zh_params(h, d):
        part = params_v.at[x, zh, c, :, half(h)]
        return remote(part, part, az_s.at[h, d - 1], az_r.at[h, d - 1], device(dzh=d))

    def x_params(h, d):
        part = params_v.at[x, :, c, :, half(h)]
        return remote(part, part, ax_s.at[h, d - 1], ax_r.at[h, d - 1], device(dx=d))

    def core_params(h):
        part = params_v.at[:, :, c, :, half(h)]
        return remote(part, part, ac_s.at[h], ac_r.at[h], device(dc=1))

    def at(b, k):
        start = b * BLOCK + k * WIDTH
        return pl.ds(start if isinstance(start, int) else pl.multiple_of(start, WIDTH), WIDTH)

    def owned(d, b, k):
        return pl.ds(
            pl.multiple_of(((y + d) % NY) * 2 * BLOCK + b * BLOCK + k * WIDTH, WIDTH), WIDTH
        )

    def turn(o, k):
        return (1 - o) * ((k + SPLIT - 1) // SPLIT) + o * ((k + 1) // SPLIT)

    def side(o, k):
        return 1 - 2 * turn(o, k)

    def far_part(o, b, k):
        return remote(
            tokens.at[:, owned(2, b, k)], far_v.at[:, at(b, k)],
            far_s.at[o, k], far_r.at[o, k], device(dy=NY - side(o, k)),
        )

    def near_part(o, b, k):
        return remote(
            tokens.at[:, owned(NY + side(o, k), b, k)], near_v.at[:, at(b, k)],
            near_s.at[o, k], near_r.at[o, k], device(dy=NY + side(o, k)),
        )

    def product_part(o, b, k):
        return remote(
            part_s.at[at(b, k)], part_v.at[at(b, k)],
            part_ss.at[o, k], part_rs.at[o, k], device(dy=NY - side(o, k)),
        )

    def cot_part(i):
        return remote(
            cot_own, cot_near.at[1 - i], cot_s.at[i], cot_r.at[1 - i], device(dy=1 + 2 * i)
        )

    def swap_part(i, d):
        col = pl.multiple_of(d * 2 * BLOCK + (1 - zl) * BLOCK + (SPLIT + i) * WIDTH, WIDTH)
        return remote(
            tokens.at[:, pl.ds(col, WIDTH)], swap_v.at[i, d],
            swap_ss.at[i, d], swap_rs.at[i, d], device(dz=1),
        )

    def cot_swap_part():
        return remote(cot_own, cot_swap, cs_s, cs_r, device(dz=1))

    def away_part(i):
        return remote(
            away_s.at[i], away_v.at[i], away_ss.at[i], away_rs.at[i],
            device(dy=NY - 1 + 2 * (i % 2)),
        )

    def side_part(i):
        return remote(
            side_s.at[i], side_v.at[i], side_ss.at[i], side_rs.at[i],
            device(dy=NY + 1 - 2 * (i % 2)),
        )

    def sum_part(i):
        return remote(
            sum_s.at[i], sum_v.at[i], sum_ss.at[i], sum_rs.at[i],
            device(dy=NY - 1 + 2 * (i % 2)),
        )

    def chunk(q):
        first, last, odd = 1 - (q + 2 * SPLIT - 1) // (2 * SPLIT), (q + 1) // (2 * SPLIT), q % 2
        o = (1 - odd) * (1 - first) + last
        k = odd * ((q + 1) // 2 - last) + (1 - odd) * (q // 2 - 1 + first)
        return o, o * zl + (1 - o) * (1 - zl), k

    def z_part(k):
        rows = pl.ds(pl.multiple_of(k * WIDTH, WIDTH), WIDTH)
        return remote(zs.at[rows], zr.at[rows], z_s.at[k], z_r.at[k], device(dz=1))

    def gain_part(i):
        part = gg_v.at[:, pl.ds(pl.multiple_of(fs * BLOCK, BLOCK), BLOCK)]
        return remote(part, part, gg_s.at[i - 1], gg_r.at[i - 1], device(dy=i // 2, dz=i % 2))


    @pl.loop(0, SPLIT)
    def _(q):
        far_part(*chunk(q)).start()

    for h in range(HALVES):
        core_sum(h).start()
    for i in range(DOWN):
        for d in range(NY):
            swap_part(i, d).start()


    local[0].wait()
    local[1].wait()

    @pl.loop(0, TOK // 16)
    def _(i):
        rows = pl.ds(pl.multiple_of(i * 16, 16), 16)
        part = tok_v[rows, :].astype(F32)
        inverse = lax.rsqrt(jnp.sum(part * part, axis=1, keepdims=True) / D + epsilon)
        cot_own[rows, :] = (cot_v[rows, :].astype(F32) * inverse).astype(BF16)

    for i in (0, 1):
        cot_part(i).start()
    cot_swap_part().start()

    @pl.loop(SPLIT, 2 * SPLIT)
    def _(q):
        far_part(*chunk(q)).start()

    @pl.loop(0, AHEAD)
    def _(q):
        near_part(*chunk(q)).start()

    local[2].wait()
    for h in range(HALVES):
        core_sum(h).wait_recv()

        @pl.loop(0, NX * NZH)
        def _(i):
            i, j = i // NZH, i % NZH
            pair_v[i, j, :, half(h)] = (
                frag_v[i, j, c, :, half(h)].astype(F32) + frag_r[i, j, :, half(h)].astype(F32)
            ).astype(BF16)

        for d in (2, 1, 3):
            x_sum(h, d).start()

    for i in (3, 4, 5, 6):
        local[i].wait()

    def s2(h):
        for d in (1, 3, 2):
            x_sum(h, d).wait_recv()

        @pl.loop(0, NZH)
        def _(j):
            total = pair_v[x, j, :, half(h)].astype(F32)
            for d in (1, 2, 3):
                total = total + xr[d - 1, j, :, half(h)].astype(F32)
            quad_v[j, :, half(h)] = total.astype(BF16)

        if h == 0:
            later_barrier()
        for d in (2, 1, 3):
            zh_sum(h, d).start()

    def s3(h):
        for d in (1, 3, 2):
            zh_sum(h, d).wait_recv()
        total = quad_v[zh, :, half(h)].astype(F32)
        for d in (1, 2, 3):
            total = total + zhr[d - 1, :, half(h)].astype(F32)
        picked = index_ref[0]
        chosen = gt_v[picked, :, half(h)]
        velocity = mt_v[picked, :, half(h)]
        delta = chosen - total / (NX * NZH * NC)
        new_velocity = outer_beta * velocity + delta
        new_params = chosen - outer_rate * (delta + outer_beta * new_velocity)
        params_v[x, zh, c, :, half(h)] = new_params.astype(BF16)
        for d in (2, 1, 3):
            zh_params(h, d).start()
        for i in range(4):
            ng_v[i, :, half(h)] = jnp.where(picked == i, new_params, gt_v[i, :, half(h)])
            nm_v[i, :, half(h)] = jnp.where(picked == i, new_velocity, mt_v[i, :, half(h)])

    def s4(h):
        for d in (1, 3, 2):
            zh_params(h, d).wait_recv()
        for d in (2, 1, 3):
            x_params(h, d).start()

    def s5(h):
        for d in (1, 3, 2):
            x_params(h, d).wait_recv()
        core_params(h).start()

    def s6(h):
        core_params(h).wait_recv()
        core_sum(h).wait_send()
        for d in (1, 2, 3):
            for part in (x_sum, zh_sum, zh_params, x_params):
                part(h, d).wait_send()
        if h > 0:
            core_params(h - 1).wait_send()

        @pl.loop(0, NX * NZH)
        def _(i):
            i, j = i // NZH, i % NZH
            nf_v[i, j, :, :, half(h)] = (
                mix_weight * frag_v[i, j, :, :, half(h)].astype(F32)
                + (1.0 - mix_weight) * params_v[i, j, :, :, half(h)].astype(F32)
            ).astype(BF16)

    for i in (0, 1):
        cot_part(1 - i).wait_recv()

    def combine(q):
        o, b, k = chunk(q)
        far_part(o, b, k).wait_recv()
        part_s[at(b, k), :] = (
            dot_rows(tok_v[:, owned(NY - side(o, k), b, k)], cot_own[...])
            + dot_rows(far_v[:, at(b, k)], cot_near[turn(o, k)])
        ).astype(BF16)
        product_part(o, b, k).start()

    def collect(o, b, k):
        near_part(o, b, k).wait_recv()
        mine = dot_rows(tok_v[:, owned(0, b, k)], cot_own[...]) + dot_rows(
            near_v[:, at(b, k)], cot_near[1 - turn(o, k)]
        )
        product_part(o, b, k).wait_recv()
        return mine + part_v[at(b, k), :].astype(F32)

    def conclude(k, total):
        rows = at(0, k)
        where = pl.ds(pl.multiple_of(fs * BLOCK + k * WIDTH, WIDTH), WIDTH)
        terms = total * weight_v[rows, :].astype(F32)
        terms = sum(terms[:, i * 128 : (i + 1) * 128] for i in range(VW // 128))
        gg_v[:, where] = jnp.sum(terms.T, axis=0, keepdims=True)
        gains = jnp.broadcast_to(gain_v[:, where], (128, WIDTH)).T
        wg_v[rows, :] = (total * jnp.concatenate([gains] * (VW // 128), axis=1)).astype(BF16)

    def sent(q):
        o, b, k = chunk(q)
        for part in (far_part, near_part, product_part):
            part(o, b, k).wait_send()

    def finish(q):
        o, _, k = chunk(q)
        rows = pl.ds(pl.multiple_of(k * WIDTH, WIDTH), WIDTH)

        @pl.when(o == 0)
        def _():
            zs[rows, :] = collect(o, 1 - zl, k).astype(BF16)
            z_part(k).start()

        @pl.when(o == 1)
        def _():
            mine = collect(o, zl, k)
            z_part(k).wait_recv()
            conclude(k, mine + zr[rows, :].astype(F32))

    def both(i, d):
        if i == 0 and d == 2:
            cot_swap_part().wait_recv()
        if d == 2:
            for e in range(NY):
                swap_part(i, e).wait_recv()
        return dot_rows(tok_v[:, owned(d, zl, SPLIT + i)], cot_own[...]) + dot_rows(
            swap_v[i, (y + d) % NY], cot_swap[...]
        )

    def away(i):
        away_s[i] = both(i, 2).astype(BF16)
        away_part(i).start()

    def beside(i):
        side_s[i] = both(i, NY + 1 - 2 * (i % 2)).astype(BF16)
        side_part(i).start()

    def pass_on(i):
        mine = both(i, NY - 1 + 2 * (i % 2))
        away_part(i).wait_recv()
        sum_s[i] = (mine + away_v[i].astype(F32)).astype(BF16)
        sum_part(i).start()

    def add_up(i):
        if i == 0:
            for j in (0, 1):
                cot_part(j).wait_send()
            cot_swap_part().wait_send()
        for d in range(NY):
            swap_part(i, d).wait_send()
        for part in (away_part, side_part):
            part(i).wait_send()
        mine = both(i, 0)
        side_part(i).wait_recv()
        sum_part(i).wait_recv()
        conclude(SPLIT + i, mine + side_v[i].astype(F32) + sum_v[i].astype(F32))

    steps = {
        1: [(s2, 0)],
        2: [(away, 0), (s2, 1)],
        3: [(s2, 2)],
        4: [(s3, 0), (away, 1), (s2, 3)],
        5: [(s3, 1), (beside, 0)],
        6: [(s3, 2), (pass_on, 0)],
        7: [(s4, 0), (s3, 3), (beside, 1)],
        8: [(s4, 1), (pass_on, 1)],
        9: [(s4, 2)],
        10: [(s4, 3), (add_up, 0)],
        11: [(s5, 0), (s5, 1), (add_up, 1)],
        12: [(s5, 2)],
        13: [(s5, 3)],
        14: [(s6, 0), (s6, 1)],
    }

    @pl.loop(0, 2 * SPLIT + LAG)
    def _(q):
        @pl.when(q < 2 * SPLIT)
        def _():
            combine(q)

            @pl.when(q + AHEAD < 2 * SPLIT)
            def _():
                near_part(*chunk(q + AHEAD)).start()

        for when, calls in steps.items():

            @pl.when(q == when)
            def _():
                for step, h in calls:
                    step(h)

        @pl.when(q >= LAG)
        def _():
            finish(q - LAG)

        @pl.when((q >= LAG) & (q < 2 * SPLIT))
        def _():
            sent(q - LAG)

    for i in (7, 3, 5, 4, 6, 2, 1):
        gain_part(i).start()
    for h in range(2, HALVES):
        s6(h)

    core_params(HALVES - 1).wait_send()
    for i in range(DOWN):
        sum_part(i).wait_send()

    @pl.loop(2 * SPLIT - LAG, 2 * SPLIT)
    def _(q):
        sent(q)

    for k in range(SPLIT):
        z_part(k).wait_send()

    for i in range(1, 8):
        gain_part(i).wait_recv()
    for i in range(1, 8):
        gain_part(i).wait_send()


def store(*refs):
    copies = [pltpu.make_async_copy(refs[i], refs[5 + i], refs[10].at[i]) for i in range(5)]
    for copy in copies:
        copy.start()
    for copy in copies:
        copy.wait()


def body(tokens, cotangent, gain, value_weight, fragment, global_table, momentum_table, frag_index):
    grid = (NX, NZH, NC, ROWS, KVW)
    dma = pltpu.SemaphoreType.DMA
    any_space = pl.BlockSpec(memory_space=pl.ANY)
    results = (
        jax.ShapeDtypeStruct((BLOCK, VW), BF16),
        jax.ShapeDtypeStruct((1, D), F32),
        jax.ShapeDtypeStruct(grid, BF16),
        jax.ShapeDtypeStruct((4, ROWS, KVW), F32),
        jax.ShapeDtypeStruct((4, ROWS, KVW), F32),
    )
    found = pl.pallas_call(
        kernel,
        out_shape=[pltpu.VMEM(r.shape, r.dtype) for r in results],
        in_specs=[pl.BlockSpec(memory_space=pltpu.SMEM)] + [any_space] * 7,
        out_specs=[pl.BlockSpec(memory_space=pltpu.VMEM)] * 5,
        scratch_shapes=[
            pltpu.VMEM((TOK, D), BF16),
            pltpu.VMEM((TOK, 2 * BLOCK), BF16),
            pltpu.VMEM((TOK, 2 * BLOCK), BF16),
            pltpu.VMEM((2 * BLOCK, VW), BF16),
            pltpu.VMEM((2 * BLOCK, VW), BF16),
            pltpu.VMEM((TOK, VW), BF16),
            pltpu.VMEM((TOK, VW), BF16),
            pltpu.VMEM((2, TOK, VW), BF16),
            pltpu.VMEM((1, D), F32),
            pltpu.VMEM((DOWN, NY, TOK, WIDTH), BF16),
            pltpu.VMEM((TOK, VW), BF16),
        ]
        + [pltpu.VMEM((DOWN, WIDTH, VW), BF16)] * 6
        + [
            pltpu.VMEM((BLOCK, VW), BF16),
            pltpu.VMEM((BLOCK, VW), BF16),
            pltpu.VMEM((BLOCK, VW), BF16),
            pltpu.VMEM(grid, BF16),
            pltpu.VMEM((NX, NZH, ROWS, KVW), BF16),
            pltpu.VMEM((NX, NZH, ROWS, KVW), BF16),
            pltpu.VMEM((NX - 1, NZH, ROWS, KVW), BF16),
            pltpu.VMEM((NZH, ROWS, KVW), BF16),
            pltpu.VMEM((NZH - 1, ROWS, KVW), BF16),
            pltpu.VMEM(grid, BF16),
        ]
        + [pltpu.VMEM((4, ROWS, KVW), F32)] * 2
        + [dma((7,))]
        + [dma((2, CHUNKS))] * 6
        + [dma((2,))] * 2
        + [dma((CHUNKS,))] * 2
        + [dma((7,))] * 2
        + [dma((DOWN, NY))] * 2
        + [dma] * 2
        + [dma((DOWN,))] * 6
        + [dma((HALVES,))] * 2
        + [dma((HALVES, 3))] * 8
        + [dma((HALVES,))] * 2,
        compiler_params=pltpu.CompilerParams(
            collective_id=0, has_side_effects=True, vmem_limit_bytes=56 << 20
        ),
        cost_estimate=pl.CostEstimate(
            flops=2 * 2 * TOK * D * VW, bytes_accessed=16 << 20, transcendentals=TOK
        ),
        name="round",
    )(
        frag_index.reshape(1),
        tokens,
        cotangent,
        gain,
        value_weight.reshape(BLOCK, VW),
        fragment.reshape(grid),
        global_table,
        momentum_table,
    )
    wg, gg, nf, ng, nm = pl.pallas_call(
        store,
        out_shape=results,
        in_specs=[any_space] * 5,
        out_specs=[any_space] * 5,
        scratch_shapes=[dma((5,))],
        compiler_params=pltpu.CompilerParams(vmem_limit_bytes=4 << 20),
        name="store",
    )(*found)
    return wg[None], gg, nf.reshape(1, BLOCK, KVW), ng, nm


def solution(mesh):
    placed = (
        P(("replica", "fsdp"), None),
        P(("replica", "fsdp"), None),
        P("replica", None),
        P("replica", "fsdp", None),
        P("replica", "fsdp", None),
        P(None, ("fsdp", "replica"), None),
        P(None, ("fsdp", "replica"), None),
        P(),
    )
    return jax.shard_map(
        body,
        mesh=mesh,
        in_specs=placed,
        out_specs=(
            P("replica", "fsdp", None),
            P("replica", None),
            P("replica", "fsdp", None),
            P(None, ("fsdp", "replica"), None),
            P(None, ("fsdp", "replica"), None),
        ),
        check_vma=False,
    )
```
